256 devices in a mesh: seq: 32 (over y, x, core), tp: 8 (over z).
Axes of the slice: x: 4, y: 4, z: 8, core: 2. Of those that a mesh axis runs over, the one named last changes fastest.
Arguments:
- queries: bfloat16 [32768, 5120], P('seq', 'tp'), may hold values from -120 to 120
- key_heads: bfloat16 [32768, 1024], P('seq', 'tp'), may hold values from -5 to 5
- token_value_heads: bfloat16 [32768, 1024], P('seq', 'tp'), may hold values from -6 to 6
- out_weight: bfloat16 [5120, 5120], P('tp'), may hold values from -0.078125 to 0.078125
- doc_lengths: int32 [8, 12], replicated, may hold values from 1 to 2048, 4096 in all within a row
- owner_of: int32 [256], replicated, may hold values from 0 to 31, as said below
Outputs:
- mixed: bfloat16 [32768, 5120], P('seq', 'tp')
The draws below stay inside these ranges and needn't reach their ends.
Inputs may be any that keep to these rules, and one draw needn't show every extreme that they name: `doc_lengths`: each row holds the lengths of its 12 documents in order, summing to 4096; the longest is exactly 2048. `owner_of`: an arbitrary placement of blocks, independent of the documents. For each b in 0..7 the blocks b of the 32 indices go to 32 different owners, so every owner holds exactly one block of each b; the 8 blocks of one index go to 8 different owners.
All inputs are finite; a program needn't handle non-finite values.
Results may differ from the reference program's by a relative error of at most 0.017.
Values may be sent and summed in bfloat16 or wider, within the bound.
A program may use at most 256 MiB of HBM per device.

```python
import math
import jax
import jax.numpy as jnp
import numpy as np
from jax import lax

D = 5120
QUERY_HEADS = 40
KEY_VALUE_HEADS = 8
HEAD_SIZE = 128
BLK = 128
LEN = 4096
NDOCS = 12
MAXDOC = 2048
BPD = 8
TOKEN_TOTAL = 32768
SEQS = 8
N_SEQ = 32
N_TP = 8


def common_draw(key):
    starting_point = jnp.clip(jax.random.normal(jax.random.fold_in(key, 101), (TOKEN_TOTAL, KEY_VALUE_HEADS * HEAD_SIZE), jnp.float32), -5.0, 5.0)
    return starting_point


def draw_key_heads(key, part):
    starting_point = common_draw(key)
    return starting_point.astype(jnp.bfloat16)


def draw_queries(key, part):
    key = jax.random.fold_in(key, 12)
    return jnp.clip(jax.random.normal(key, (TOKEN_TOTAL, QUERY_HEADS * HEAD_SIZE), jnp.float32), -5.0, 5.0).astype(jnp.bfloat16)


def draw_owner_of(key, part):
    key = jax.random.fold_in(key, 13)
    first_key, second_key, third_key = jax.random.split(key, 3)
    relabel = jax.random.permutation(first_key, N_SEQ)
    rotation = jax.random.permutation(second_key, N_SEQ)
    offsets = jnp.take(jax.random.permutation(third_key, N_SEQ), jnp.arange(BPD) % N_SEQ)
    slot_index = (rotation[:, None] + offsets[None, :]) % N_SEQ
    return relabel[slot_index].reshape(N_SEQ * BPD).astype(jnp.int32)


def block_scale(rng, dims, cuts, low, largest):
    level = 1.0
    for position, parts in cuts:
        steps = jax.random.uniform(jax.random.fold_in(jax.random.fold_in(rng, 6), position), (parts,), jnp.float32, low / len(cuts), largest / len(cuts))
        level = level * jnp.repeat(jnp.exp(steps), dims[position] // parts).reshape((-1,) + (1,) * (len(dims) - 1 - position))
    return level


def split_up(count, total, most, lean):
    portions = [(1 << 20) // math.isqrt(grade ** lean) + 1 for grade in range(2, count + 1)]
    rest, given = total - most - (count - 1), [1] * (count - 1)
    while rest > 0:
        free = [i for i in range(count - 1) if given[i] < most]
        pool, budget = sum([portions[i] for i in free]), rest
        for i in free:
            addition = min(most - given[i], max(1, budget * portions[i] // pool), rest)
            given[i] = given[i] + addition
            rest = rest - addition
    return np.array([most] + given)


def ragged_sizes(stream_key, number_of, total, reach, lean):
    if number_of == 2:
        one = jax.random.randint(stream_key, (), max(1, total - reach), min(reach, total - 1) + 1)
        return jnp.stack([one, total - one])
    tallies = jnp.asarray(split_up(number_of, total, reach, lean), jnp.int32)
    couples = (number_of - 1) // 2
    source_of, receiver = tallies[1:1 + 2 * couples:2], tallies[2:2 + 2 * couples:2]
    margin = jnp.minimum(source_of - 1, reach - receiver)
    passed = jax.random.randint(jax.random.fold_in(stream_key, 1), (couples,), 0, 1 << 20) % (margin + 1)
    tallies = tallies.at[1:1 + 2 * couples:2].set(source_of - passed).at[2:2 + 2 * couples:2].set(receiver + passed)
    return tallies[jax.random.permutation(jax.random.fold_in(stream_key, 2), number_of)]


def gaussian(stream_key, dims, deviation, most, shards=(), kind=jnp.bfloat16):
    gain = block_scale(stream_key, dims, shards, -0.22, 0.18) if shards else 1.0
    values = jax.random.normal(stream_key, dims, jnp.float32) * deviation * gain
    return jnp.minimum(jnp.maximum(values, -most), most).astype(kind)


def setup_inputs(seed: int = 0) -> dict:
    arg_keys = jax.random.split(jax.random.key(seed), 7)
    return {
        "queries": draw_queries(jax.random.fold_in(arg_keys[6], 71), 0),
        "key_heads": draw_key_heads(jax.random.fold_in(arg_keys[6], 71), 0),
        "token_value_heads": gaussian(arg_keys[2], (TOKEN_TOTAL, KEY_VALUE_HEADS * HEAD_SIZE), 1.0, 6.0, ((0, 32), (1, 8))),
        "out_weight": gaussian(arg_keys[3], (QUERY_HEADS * HEAD_SIZE, D), (QUERY_HEADS * HEAD_SIZE) ** -0.5, 0.078125, ((0, 8),)),
        "doc_lengths": jax.vmap(lambda own: ragged_sizes(own, NDOCS, LEN, MAXDOC, 2))(jax.random.split(arg_keys[4], SEQS)).reshape((SEQS, NDOCS)).astype(jnp.int32),
        "owner_of": draw_owner_of(jax.random.fold_in(arg_keys[6], 71), 0),
    }


floor_score = -1e+30

def doc_ids(doc_lengths, positions):
    seq_count, doc_count = doc_lengths.shape
    sequence_id = (positions // LEN).astype(jnp.int32)
    inner_pos = (positions - sequence_id * LEN).astype(jnp.int32)
    doc_bounds = jnp.cumsum(doc_lengths, axis=1).astype(jnp.int32)
    chosen = (sequence_id[:, None] == jnp.arange(seq_count, dtype=jnp.int32)[None, :]).astype(jnp.int32)
    row_bounds = lax.optimization_barrier(jnp.sum(chosen[:, :, None] * doc_bounds[None, :, :], axis=1)).astype(jnp.int32)
    docs_before = lax.optimization_barrier(jnp.sum((inner_pos[:, None] >= row_bounds).astype(jnp.int32), axis=1)).astype(jnp.int32)
    return (sequence_id * doc_count + docs_before).astype(jnp.int32)

def reference(queries, key_heads, token_value_heads, out_weight, doc_lengths, owner_of):
    total_tokens, feature_width = queries.shape
    kv_width = key_heads.shape[1]
    kv_count = kv_width // HEAD_SIZE
    group_size = feature_width // kv_width
    block_count = total_tokens // BLK
    score_scale = 1.0 / math.sqrt(HEAD_SIZE)
    window = MAXDOC + BLK

    def one_block(block_index):
        first = (block_index * BLK).astype(jnp.int32)
        key_first = jnp.clip(first + BLK - window, 0, total_tokens - window).astype(jnp.int32)
        query_block = lax.dynamic_slice_in_dim(queries, first, BLK, 0).astype(jnp.float32)
        query_block = query_block.reshape(BLK, kv_count, group_size, HEAD_SIZE)
        keys_near = lax.dynamic_slice_in_dim(key_heads, key_first, window, 0).astype(jnp.float32)
        keys_near = keys_near.reshape(window, kv_count, HEAD_SIZE)
        values_near = lax.dynamic_slice_in_dim(token_value_heads, key_first, window, 0).astype(jnp.float32)
        values_near = values_near.reshape(window, kv_count, HEAD_SIZE)
        scores = jnp.einsum('qhgd,khd->hgqk', query_block, keys_near, precision=lax.Precision.HIGHEST) * score_scale
        query_pos = first + jnp.arange(BLK, dtype=jnp.int32)
        key_pos = key_first + jnp.arange(window, dtype=jnp.int32)
        allowed = (doc_ids(doc_lengths, query_pos)[:, None] == doc_ids(doc_lengths, key_pos)[None, :]) & (key_pos[None, :] <= query_pos[:, None])
        scores = jnp.where(allowed[None, None], scores, floor_score)
        row_max = lax.optimization_barrier(jnp.max(scores, axis=-1))
        weights = jnp.where(allowed[None, None], jnp.exp(scores - row_max[..., None]), 0.0)
        row_sum = lax.optimization_barrier(jnp.sum(weights, axis=-1))
        rounded = lax.optimization_barrier(weights.astype(jnp.bfloat16))
        numer = jnp.einsum('hgqk,khd->hgqd', rounded.astype(jnp.float32), values_near, precision=lax.Precision.HIGHEST)
        result = numer / row_sum[..., None]
        return jnp.transpose(result, (2, 0, 1, 3)).reshape(BLK, feature_width).astype(jnp.bfloat16)
    attended = lax.map(one_block, jnp.arange(block_count, dtype=jnp.int32))
    block_ids = jnp.arange(block_count, dtype=jnp.int32)
    slots = (owner_of * BPD + block_ids % BPD).astype(jnp.int32)
    source = jnp.zeros((block_count,), jnp.int32).at[slots].set(block_ids)
    placed = attended[source].reshape(total_tokens, feature_width)
    part_width = feature_width // N_TP
    result = jnp.zeros((total_tokens, out_weight.shape[1]), jnp.float32)
    for group_index in range(N_TP):
        columns = placed[:, group_index * part_width:(group_index + 1) * part_width]
        rows_part = out_weight[group_index * part_width:(group_index + 1) * part_width]
        partial_value = jnp.dot(columns, rows_part, preferred_element_type=jnp.float32).astype(jnp.bfloat16)
        partial_value = lax.optimization_barrier(partial_value)
        result = result + partial_value.astype(jnp.float32)
    return result.astype(jnp.bfloat16)
```

```python
import functools
import math

import jax
import jax.numpy as jnp
from jax import lax
from jax.experimental import pallas as pl
from jax.experimental.pallas import tpu as pltpu
from jax.sharding import PartitionSpec as P

HEAD_SIZE = 128
BLK = 128
LEN = 4096
MAXDOC = 2048
HEADS = 5
ROWS = 1024
WIDTH = HEADS * HEAD_SIZE
BLOCKS = ROWS // BLK
WINDOW = MAXDOC + BLK
SEQ = 32
TP = 8
PER_SEQ = LEN // ROWS
QUARTER = BLK // 4
X_ROWS = 384
X_PIECE = 48
Y_PIECE = 32
MESH = pl.DeviceIdType.MESH

D_PROJ = 4
D_FAR = 5
D_FINAL = 7
D_MID = 9


def pair_of(z):
    return lax.rem(z + jnp.where(lax.rem(z, 2) == 1, 1, TP - 1), TP)


def buddy_of(z):
    return z + 1 - 2 * lax.rem(z, 2)


def far_of(z):
    return lax.rem(z + jnp.where(lax.rem(z, 2) == 1, 3, 5), TP)


def slot_column(z, slot):
    base = jnp.where(slot >= 2, buddy_of(z), z)
    return jnp.where(lax.rem(slot, 2) == 1, far_of(base), base)


def middle_of(block, quarter):
    return (quarter * 4 + lax.rem(block + quarter, 4)) * 2 + block // 4


def kernel(
    doc_ref,
    inverse_ref,
    q_ref,
    k_hbm,
    v_hbm,
    w_hbm,
    out_ref,
    kbuf,
    vbuf,
    weight,
    att,
    part,
    brecv,
    fsend,
    frecv,
    mixed,
    midr,
    mids,
    local_sem,
    kv_send,
    kv_recv,
    w_send,
    w_recv,
    pair_send,
    pair_recv,
    buddy_send,
    buddy_recv,
    far_send,
    far_recv,
    route_send,
    mid_recv,
    mid_send,
    out_recv,
):
    me = lax.axis_index("seq")
    z = lax.axis_index("tp")
    core = lax.rem(me, 2)
    x = lax.rem(me // 2, 4)
    y = me // 8
    j = lax.rem(me, PER_SEQ)
    pair, buddy, far = pair_of(z), buddy_of(z), far_of(z)
    scale = math.log2(math.e) / math.sqrt(HEAD_SIZE)

    def remote(src, dst, send, recv, target):
        return pltpu.make_async_remote_copy(
            src_ref=src,
            dst_ref=dst,
            send_sem=send,
            recv_sem=recv,
            device_id=target,
            device_id_type=MESH,
        )

    own_k = pltpu.make_async_copy(k_hbm, kbuf.at[pl.ds(2 * ROWS, ROWS)], local_sem.at[0])
    own_v = pltpu.make_async_copy(v_hbm, vbuf.at[pl.ds(2 * ROWS, ROWS)], local_sem.at[1])
    own_k.start()
    own_v.start()

    def own_weight(slot):
        column = pl.multiple_of(slot_column(z, slot) * WIDTH, WIDTH)
        return pltpu.make_async_copy(
            w_hbm.at[:, pl.ds(column, WIDTH)],
            weight.at[pl.ds(0, WIDTH), pl.ds(slot * WIDTH, WIDTH)],
            local_sem.at[2 + slot],
        )

    for slot in range(4):
        own_weight(slot).start()

    barrier = pltpu.get_barrier_semaphore()

    @pl.loop(1, SEQ)
    def _(step):
        pl.semaphore_signal(
            barrier, inc=1, device_id={"seq": lax.rem(me + step, SEQ)}, device_id_type=MESH
        )

    for target in (pair, buddy, far):
        pl.semaphore_signal(barrier, inc=1, device_id={"tp": target}, device_id_type=MESH)
    pl.semaphore_wait(barrier, SEQ - 1 + 3)

    rp = core * 4 + x

    def x_rows(which):
        return pl.ds(pl.multiple_of(WIDTH + which * X_PIECE, 16), X_PIECE)

    def y_rows(which):
        return pl.ds(pl.multiple_of(WIDTH + X_ROWS + which * Y_PIECE, 16), Y_PIECE)

    def slot_cols(which):
        return pl.ds(pl.multiple_of(which * WIDTH, WIDTH), WIDTH)

    theirs = pl.ds(pl.multiple_of(slot_column(pair, y) * WIDTH, WIDTH), WIDTH)

    def w_first(part_no):
        if part_no == 0:
            src = w_hbm.at[pl.ds(pl.multiple_of(rp * X_PIECE, 16), X_PIECE), theirs]
            dst = weight.at[x_rows(rp), slot_cols(y)]
        else:
            src = w_hbm.at[pl.ds(pl.multiple_of(X_ROWS + rp * Y_PIECE, 16), Y_PIECE), theirs]
            dst = weight.at[y_rows(rp), slot_cols(y)]
        return remote(src, dst, w_send.at[part_no], w_recv.at[part_no], {"tp": pair})

    def along_x(step):
        return {"seq": (y * 4 + lax.rem(x + step, 4)) * 2 + core}

    def along_y(step):
        return {"seq": (lax.rem(y + step, 4) * 4 + x) * 2 + core}

    def w_second(part_no, step):
        sem = 2 + part_no * 3 + step - 1
        if part_no == 0:
            ref, target = weight.at[x_rows(rp), slot_cols(y)], along_x(step)
        else:
            ref, target = weight.at[y_rows(rp), slot_cols(y)], along_y(step)
        return remote(ref, ref, w_send.at[sem], w_recv.at[sem], target)

    def w_third(part_no, step):
        sem = 8 + part_no * 3 + step - 1
        if part_no == 0:
            rows = pl.ds(pl.multiple_of(WIDTH + core * 4 * X_PIECE, 16), 4 * X_PIECE)
            ref, target = weight.at[rows, slot_cols(y)], along_y(step)
        else:
            ref, target = weight.at[y_rows(rp), :], along_x(step)
        return remote(ref, ref, w_send.at[sem], w_recv.at[sem], target)

    def w_fourth(part_no):
        sem = 14 + part_no
        if part_no == 0:
            rows = pl.ds(pl.multiple_of(WIDTH + core * 4 * X_PIECE, 16), 4 * X_PIECE)
        else:
            rows = pl.ds(pl.multiple_of(WIDTH + X_ROWS + core * 4 * Y_PIECE, 16), 4 * Y_PIECE)
        ref = weight.at[rows, :]
        return remote(ref, ref, w_send.at[sem], w_recv.at[sem], {"seq": me + 1 - 2 * core})

    w_first(0).start()
    w_first(1).start()

    def near_kv(which):
        src, buf = ((k_hbm, kbuf), (v_hbm, vbuf))[which]
        return remote(
            src,
            buf.at[pl.ds(ROWS, ROWS)],
            kv_send.at[which, BLOCKS],
            kv_recv.at[which, BLOCKS],
            {"seq": lax.rem(me + 1, SEQ)},
        )

    def next_kv(which, piece):
        src, buf = ((k_hbm, kbuf), (v_hbm, vbuf))[which]
        rows = pl.ds(pl.multiple_of(piece * BLK, BLK), BLK)
        return remote(
            src.at[rows],
            buf.at[rows],
            kv_send.at[which, piece],
            kv_recv.at[which, piece],
            {"seq": lax.rem(me + 2, SEQ)},
        )

    @pl.when(j < 3)
    def _():
        near_kv(0).start()
        near_kv(1).start()

    @pl.when(j < 2)
    def _():
        @pl.loop(0, BLOCKS)
        def _(step):
            next_kv(0, BLOCKS - 1 - step).start()
            next_kv(1, BLOCKS - 1 - step).start()

        kbuf[pl.ds(0, ROWS), :] = jnp.zeros((ROWS, HEAD_SIZE), kbuf.dtype)
        vbuf[pl.ds(0, ROWS), :] = jnp.zeros((ROWS, HEAD_SIZE), vbuf.dtype)

    @pl.when(j < 1)
    def _():
        kbuf[pl.ds(ROWS, ROWS), :] = jnp.zeros((ROWS, HEAD_SIZE), kbuf.dtype)
        vbuf[pl.ds(ROWS, ROWS), :] = jnp.zeros((ROWS, HEAD_SIZE), vbuf.dtype)

    def rows_of(block):
        return pl.ds(pl.multiple_of(block * BLK, BLK), BLK)

    def pair_copy(block):
        rows = rows_of(block)
        return remote(
            att.at[rows, pl.ds(0, WIDTH)],
            att.at[rows, pl.ds(WIDTH, WIDTH)],
            pair_send.at[block],
            pair_recv.at[block],
            {"tp": pair},
        )

    def buddy_copy(block):
        rows = rows_of(block)
        return remote(
            part.at[rows, pl.ds(2 * WIDTH, 2 * WIDTH)],
            brecv.at[rows],
            buddy_send.at[block],
            buddy_recv.at[block],
            {"tp": buddy},
        )

    def far_copy(block):
        rows = rows_of(block)
        return remote(
            fsend.at[rows], frecv.at[rows], far_send.at[block], far_recv.at[block], {"tp": far}
        )

    def attention(block):
        rows = rows_of(block)
        window = pl.ds(pl.multiple_of(block * BLK, BLK), WINDOW)
        keys = kbuf[window, :]
        values = vbuf[window, :]
        base = j * ROWS + block * BLK
        position = base + lax.broadcasted_iota(jnp.int32, (BLK, 1), 0)
        bound = jnp.int32(0)
        first = jnp.zeros((BLK, 1), jnp.int32)
        for doc in range(doc_ref.shape[1]):
            bound = bound + doc_ref[me // PER_SEQ, doc]
            first = jnp.where(position >= bound, bound, first)
        first = first - base + MAXDOC
        key_no = lax.broadcasted_iota(jnp.int32, (BLK, WINDOW), 1)
        last = MAXDOC + lax.broadcasted_iota(jnp.int32, (BLK, WINDOW), 0)
        allowed = (key_no >= first) & (key_no <= last)
        for head in range(HEADS):
            columns = pl.ds(head * HEAD_SIZE, HEAD_SIZE)
            scores = lax.dot_general(
                q_ref[rows, columns],
                keys,
                (((1,), (1,)), ((), ())),
                preferred_element_type=jnp.float32,
            )
            scores = jnp.where(allowed, scores * scale, -1e30)
            weights = jnp.exp2(scores - jnp.max(scores, axis=1, keepdims=True))
            total = jnp.sum(weights, axis=1, keepdims=True)
            mix = jnp.dot(
                weights.astype(jnp.bfloat16), values, preferred_element_type=jnp.float32
            )
            att[rows, columns] = (mix / total).astype(jnp.bfloat16)

    def project(block, slots):
        rows = rows_of(block)
        for slot in slots:
            columns = pl.ds(slot * WIDTH, WIDTH)
            part[rows, columns] = jnp.dot(
                att[rows, :], weight[:, columns], preferred_element_type=jnp.float32
            ).astype(jnp.bfloat16)

    def route_copy(block, quarter, target):
        rows = pl.ds(pl.multiple_of(block * BLK + quarter * QUARTER, QUARTER), QUARTER)
        return remote(
            mixed.at[rows], midr.at[me], route_send.at[block, quarter], mid_recv, {"seq": target}
        )

    my_quarter = y
    my_block = core * 4 + lax.rem(x + 4 - y, 4)
    my_rows = pl.ds(pl.multiple_of(my_block * BLK + my_quarter * QUARTER, QUARTER), QUARTER)

    def mid_copy(target):
        return remote(
            mids.at[target],
            out_ref.at[my_rows],
            mid_send.at[target],
            out_recv.at[my_block],
            {"seq": target},
        )

    own_mid = pltpu.make_async_copy(mixed.at[my_rows], midr.at[me], mid_recv)
    own_out = pltpu.make_async_copy(mids.at[me], out_ref.at[my_rows], out_recv.at[my_block])

    @pl.loop(0, BLOCKS + D_MID)
    def _(step):
        @pl.when(step == 0)
        def _():
            own_k.wait()
            own_v.wait()

            @pl.when(j >= 1)
            def _():
                near_kv(0).wait_recv()
                near_kv(1).wait_recv()

        @pl.when(step == 1)
        def _():
            for no in range(2):
                w_first(no).wait_recv()
                for hop in (1, 3, 2):
                    w_second(no, hop).start()

        @pl.when(step == 2)
        def _():
            for no in range(2):
                for hop in (1, 3, 2):
                    w_second(no, hop).wait_recv()
                for hop in (1, 3, 2):
                    w_third(no, hop).start()

        @pl.when(step == 3)
        def _():
            for no in range(2):
                for hop in (1, 3, 2):
                    w_third(no, hop).wait_recv()
                w_fourth(no).start()

        @pl.when(step == D_PROJ)
        def _():
            for slot in range(4):
                own_weight(slot).wait()
            for no in range(2):
                w_fourth(no).wait_recv()

        @pl.when((step >= D_PROJ) & (step < D_PROJ + BLOCKS))
        def _():
            block = BLOCKS - 1 - (step - D_PROJ)
            pair_copy(block).wait_recv()
            project(block, (2, 3))
            buddy_copy(block).start()
            project(block, (1, 0))

        @pl.when((step >= D_FAR) & (step < D_FAR + BLOCKS))
        def _():
            block = BLOCKS - 1 - (step - D_FAR)
            rows = rows_of(block)
            buddy_copy(block).wait_recv()
            columns = pl.ds(WIDTH, WIDTH)
            fsend[rows, :] = (
                part[rows, columns].astype(jnp.float32) + brecv[rows, columns].astype(jnp.float32)
            ).astype(jnp.bfloat16)
            far_copy(block).start()

        @pl.when(step < BLOCKS)
        def _():
            block = BLOCKS - 1 - step

            @pl.when(j >= 2)
            def _():
                next_kv(0, block).wait_recv()
                next_kv(1, block).wait_recv()

            attention(block)
            pair_copy(block).start()

        @pl.when((step >= D_FINAL) & (step < D_FINAL + BLOCKS))
        def _():
            block = BLOCKS - 1 - (step - D_FINAL)
            rows = rows_of(block)
            far_copy(block).wait_recv()
            columns = pl.ds(0, WIDTH)
            mixed[rows, :] = (
                part[rows, columns].astype(jnp.float32)
                + brecv[rows, columns].astype(jnp.float32)
                + frecv[rows, :].astype(jnp.float32)
            ).astype(jnp.bfloat16)
            for quarter in range(4):
                target = middle_of(block, quarter)

                @pl.when(target != me)
                def _():
                    route_copy(block, quarter, target).start()

                @pl.when(target == me)
                def _():
                    own_mid.start()

        @pl.when(BLOCKS - 1 - (step - D_MID) == my_block)
        def _():
            pltpu.make_async_copy(midr, midr, mid_recv).wait()

            @pl.loop(0, SEQ)
            def _(owner):
                mids[owner] = midr[inverse_ref[my_block * SEQ + owner]]

                @pl.when(owner != me)
                def _():
                    mid_copy(owner).start()

                @pl.when(owner == me)
                def _():
                    own_out.start()

    for block in range(BLOCKS):
        rows = pl.ds(block * BLK, BLK)
        pltpu.make_async_copy(out_ref.at[rows], out_ref.at[rows], out_recv.at[block]).wait()

    @pl.when(j < 3)
    def _():
        near_kv(0).wait_send()
        near_kv(1).wait_send()

    @pl.when(j < 2)
    def _():
        @pl.loop(0, BLOCKS)
        def _(piece):
            next_kv(0, piece).wait_send()
            next_kv(1, piece).wait_send()

    for no in range(2):
        w_first(no).wait_send()
        w_fourth(no).wait_send()
        for hop in (1, 2, 3):
            w_second(no, hop).wait_send()
            w_third(no, hop).wait_send()

    @pl.loop(0, BLOCKS)
    def _(block):
        pair_copy(block).wait_send()
        buddy_copy(block).wait_send()
        far_copy(block).wait_send()
        for quarter in range(4):
            target = middle_of(block, quarter)

            @pl.when(target != me)
            def _():
                route_copy(block, quarter, target).wait_send()

    @pl.loop(0, SEQ)
    def _(owner):
        @pl.when(owner != me)
        def _():
            mid_copy(owner).wait_send()


def body(queries, key_heads, token_value_heads, out_weight, doc_lengths, owner_of):
    owner_table = owner_of.reshape(SEQ, BLOCKS)
    index = jnp.arange(SEQ, dtype=jnp.int32)
    inverse = jnp.sum(
        jnp.where(owner_table.T[:, None, :] == index[None, :, None], index[None, None, :], 0),
        axis=2,
    ).reshape(BLOCKS * SEQ)
    dma = pltpu.SemaphoreType.DMA
    bf16 = jnp.bfloat16
    any_space = pl.BlockSpec(memory_space=pl.ANY)
    smem = pl.BlockSpec(memory_space=pltpu.SMEM)
    vmem = pl.BlockSpec(memory_space=pltpu.VMEM)
    return pl.pallas_call(
        kernel,
        out_shape=jax.ShapeDtypeStruct((ROWS, WIDTH), bf16),
        in_specs=[smem, smem, vmem, any_space, any_space, any_space],
        out_specs=any_space,
        scratch_shapes=[
            pltpu.VMEM((3 * ROWS, HEAD_SIZE), bf16),
            pltpu.VMEM((3 * ROWS, HEAD_SIZE), bf16),
            pltpu.VMEM((2 * WIDTH, 4 * WIDTH), bf16),
            pltpu.VMEM((ROWS, 2 * WIDTH), bf16),
            pltpu.VMEM((ROWS, 4 * WIDTH), bf16),
            pltpu.VMEM((ROWS, 2 * WIDTH), bf16),
            pltpu.VMEM((ROWS, WIDTH), bf16),
            pltpu.VMEM((ROWS, WIDTH), bf16),
            pltpu.VMEM((ROWS, WIDTH), bf16),
            pltpu.VMEM((SEQ, QUARTER, WIDTH), bf16),
            pltpu.VMEM((SEQ, QUARTER, WIDTH), bf16),
            dma((6,)),
            dma((2, BLOCKS + 1)),
            dma((2, BLOCKS + 1)),
            dma((16,)),
            dma((16,)),
            dma((BLOCKS,)),
            dma((BLOCKS,)),
            dma((BLOCKS,)),
            dma((BLOCKS,)),
            dma((BLOCKS,)),
            dma((BLOCKS,)),
            dma((BLOCKS, 4)),
            dma,
            dma((SEQ,)),
            dma((BLOCKS,)),
        ],
        compiler_params=pltpu.CompilerParams(
            collective_id=0, has_side_effects=True, vmem_limit_bytes=56 * 1024 * 1024
        ),
        cost_estimate=pl.CostEstimate(
            flops=20_000_000_000, bytes_accessed=12_000_000, transcendentals=11_000_000
        ),
    )(doc_lengths, inverse, queries, key_heads, token_value_heads, out_weight)


def solution(mesh):
    return jax.shard_map(
        body,
        mesh=mesh,
        in_specs=(P("seq", "tp"), P("seq", "tp"), P("seq", "tp"), P("tp", None), P(), P()),
        out_specs=P("seq", "tp"),
        check_vma=False,
    )
```

```python
import functools
import math

import jax
import jax.numpy as jnp
from jax import lax
from jax.experimental import pallas as pl
from jax.experimental.pallas import tpu as pltpu
from jax.sharding import PartitionSpec as P

HEAD_SIZE = 128
BLK = 128
LEN = 4096
MAXDOC = 2048
HEADS = 5
ROWS = 1024
WIDTH = HEADS * HEAD_SIZE
BLOCKS = ROWS // BLK
WINDOW = MAXDOC + BLK
SEQ = 32
TP = 8
PER_SEQ = LEN // ROWS
PIECES = 8
PIECE = BLK // PIECES
W_PIECE = 64
W_ROWS = 4 * WIDTH + 128
MESH = pl.DeviceIdType.MESH

HALF = BLOCKS // 2

D_FORWARD = 2
D_PROJ = 4
D_FINAL = 5
D_MID = 6


def block_at(place):
    late = jnp.where(place == 7, 0, 13 - 2 * place)
    return jnp.where(place < HALF, jnp.where(place == 0, 7, 8 - 2 * place), late)


def pair_of(z):
    return lax.rem(z + jnp.where(lax.rem(z, 2) == 1, 1, TP - 1), TP)


def buddy_of(z):
    return z + 1 - 2 * lax.rem(z, 2)


def far_of(z):
    return lax.rem(z + jnp.where(lax.rem(z, 2) == 1, 3, 5), TP)


def middle_of(place, piece):
    y = piece // 2
    x = 2 * (piece % 2) + lax.rem(y + place, 2)
    return (y * 4 + x) * 2 + lax.rem(place // 2, 2)


def kernel(
    doc_ref,
    inverse_ref,
    q_ref,
    k_hbm,
    v_hbm,
    w_hbm,
    out_ref,
    kbuf,
    vbuf,
    weight,
    att,
    psend,
    precv,
    own_part,
    attended,
    mixed,
    midr_low,
    midr_high,
    mids,
    local_sem,
    kv_send,
    kv_recv,
    w_send,
    w_recv,
    own_send,
    own_recv,
    far_send,
    far_recv,
    forward_send,
    forward_recv,
    pair_send,
    pair_recv,
    route_send,
    mid_recv,
    mid_send,
    placed_recv,
    out_recv,
):
    midr = (midr_low, midr_high)
    me = lax.axis_index("seq")
    z = lax.axis_index("tp")
    core = lax.rem(me, 2)
    x = lax.rem(me // 2, 4)
    y = me // 8
    j = lax.rem(me, PER_SEQ)
    pair, buddy, far = pair_of(z), buddy_of(z), far_of(z)
    far_buddy = buddy_of(far)
    scale = math.log2(math.e) / math.sqrt(HEAD_SIZE)

    def remote(src, dst, send, recv, target):
        return pltpu.make_async_remote_copy(
            src_ref=src,
            dst_ref=dst,
            send_sem=send,
            recv_sem=recv,
            device_id=target,
            device_id_type=MESH,
        )

    own_k = pltpu.make_async_copy(k_hbm, kbuf.at[pl.ds(2 * ROWS, ROWS)], local_sem.at[0])
    own_v = pltpu.make_async_copy(v_hbm, vbuf.at[pl.ds(2 * ROWS, ROWS)], local_sem.at[1])
    own_k.start()
    own_v.start()

    def own_weight(half):
        column = pl.multiple_of((pair if half else z) * WIDTH, WIDTH)
        return pltpu.make_async_copy(
            w_hbm.at[:, pl.ds(column, WIDTH)],
            weight.at[pl.ds(0, WIDTH), pl.ds(half * WIDTH, WIDTH)],
            local_sem.at[2 + half],
        )

    for half in range(2):
        own_weight(half).start()

    barrier = pltpu.get_barrier_semaphore()

    @pl.loop(1, SEQ)
    def _(step):
        pl.semaphore_signal(
            barrier, inc=1, device_id={"seq": lax.rem(me + step, SEQ)}, device_id_type=MESH
        )

    for target in (pair, buddy, far, far_buddy):
        pl.semaphore_signal(barrier, inc=1, device_id={"tp": target}, device_id_type=MESH)
    pl.semaphore_wait(barrier, SEQ - 1 + 4)

    piece_no = (core * 4 + y) * 4 + x
    group = jnp.minimum(piece_no // 10, 2)
    w_target = jnp.where(group == 0, buddy, jnp.where(group == 1, far, far_buddy))

    def w_rows(yy, xx):
        start = WIDTH + ((core * 4 + yy) * 4 + xx) * W_PIECE
        return pl.ds(pl.multiple_of(start, W_PIECE), W_PIECE)

    def w_half(half):
        return pl.ds(half * WIDTH, WIDTH)

    def w_first(half):
        column = pair_of(w_target) if half else w_target
        src = w_hbm.at[
            pl.ds(pl.multiple_of(lax.rem(piece_no, 10) * W_PIECE, W_PIECE), W_PIECE),
            pl.ds(pl.multiple_of(column * WIDTH, WIDTH), WIDTH),
        ]
        dst = weight.at[w_rows(y, x), w_half(half)]
        return remote(src, dst, w_send.at[half], w_recv.at[half], {"tp": w_target})

    def along_x(hop):
        return {"seq": (y * 4 + lax.rem(x + hop, 4)) * 2 + core}

    def along_y(hop):
        return {"seq": (lax.rem(y + hop, 4) * 4 + x) * 2 + core}

    def w_second(half, hop):
        sem = 2 + half * 3 + hop - 1
        ref = weight.at[w_rows(y, x), w_half(half)]
        target = along_y(hop) if half else along_x(hop)
        return remote(ref, ref, w_send.at[sem], w_recv.at[sem], target)

    four_rows = pl.ds(pl.multiple_of(WIDTH + (core * 4 + y) * 4 * W_PIECE, W_PIECE), 4 * W_PIECE)

    def w_third(half, hop):
        sem = 8 + half * 3 + hop - 1
        ref = weight.at[four_rows, w_half(half)]
        target = along_x(hop) if half else along_y(hop)
        return remote(ref, ref, w_send.at[sem], w_recv.at[sem], target)

    def w_third_piece(hop, yy):
        sem = 11 + hop - 1
        ref = weight.at[w_rows(yy, x), w_half(1)]
        return remote(ref, ref, w_send.at[sem], w_recv.at[sem], along_x(hop))

    def w_fourth(half):
        sem = 14 + half
        rows = pl.ds(pl.multiple_of(WIDTH + core * 16 * W_PIECE, W_PIECE), 16 * W_PIECE)
        ref = weight.at[rows, w_half(half)]
        return remote(ref, ref, w_send.at[sem], w_recv.at[sem], {"seq": me + 1 - 2 * core})

    w_first(0).start()
    w_first(1).start()

    def near_kv(which):
        src, buf = ((k_hbm, kbuf), (v_hbm, vbuf))[which]
        return remote(
            src,
            buf.at[pl.ds(ROWS, ROWS)],
            kv_send.at[which, BLOCKS],
            kv_recv.at[which, BLOCKS],
            {"seq": lax.rem(me + 1, SEQ)},
        )

    def next_kv(which, piece):
        src, buf = ((k_hbm, kbuf), (v_hbm, vbuf))[which]
        rows = pl.ds(pl.multiple_of(piece * BLK, BLK), BLK)
        return remote(
            src.at[rows],
            buf.at[rows],
            kv_send.at[which, piece],
            kv_recv.at[which, piece],
            {"seq": lax.rem(me + 2, SEQ)},
        )

    @pl.when(j < 3)
    def _():
        near_kv(0).start()
        near_kv(1).start()

    @pl.when(j < 2)
    def _():
        next_kv(0, BLOCKS - 1).start()
        next_kv(1, BLOCKS - 1).start()
        kbuf[pl.ds(0, ROWS), :] = jnp.zeros((ROWS, HEAD_SIZE), kbuf.dtype)
        vbuf[pl.ds(0, ROWS), :] = jnp.zeros((ROWS, HEAD_SIZE), vbuf.dtype)

    @pl.when(j < 1)
    def _():
        kbuf[pl.ds(ROWS, ROWS), :] = jnp.zeros((ROWS, HEAD_SIZE), kbuf.dtype)
        vbuf[pl.ds(ROWS, ROWS), :] = jnp.zeros((ROWS, HEAD_SIZE), vbuf.dtype)

    def rows_of(block):
        return pl.ds(pl.multiple_of(block * BLK, BLK), BLK)

    def slot(no):
        return pl.ds(no * WIDTH, WIDTH)

    def own_copy(block):
        rows = rows_of(block)
        return remote(
            att.at[rows, slot(0)],
            att.at[rows, slot(1)],
            own_send.at[block],
            own_recv.at[block],
            {"tp": buddy},
        )

    def far_copy(block):
        rows = rows_of(block)
        return remote(
            att.at[rows, slot(0)],
            att.at[rows, slot(2)],
            far_send.at[block],
            far_recv.at[block],
            {"tp": far},
        )

    def forward_copy(block):
        rows = rows_of(block)
        return remote(
            att.at[rows, slot(2)],
            att.at[rows, slot(3)],
            forward_send.at[block],
            forward_recv.at[block],
            {"tp": buddy},
        )

    def pair_copy(block):
        rows = rows_of(block)
        return remote(
            psend.at[rows], precv.at[rows], pair_send.at[block], pair_recv.at[block], {"tp": pair}
        )

    def attention(place):
        block = block_at(place)
        rows = rows_of(block)
        window = pl.ds(pl.multiple_of(block * BLK, BLK), WINDOW)
        keys = kbuf[window, :]
        values = vbuf[window, :]
        base = j * ROWS + block * BLK
        position = base + lax.broadcasted_iota(jnp.int32, (BLK, 1), 0)
        bound = jnp.int32(0)
        first = jnp.zeros((BLK, 1), jnp.int32)
        for doc in range(doc_ref.shape[1]):
            bound = bound + doc_ref[me // PER_SEQ, doc]
            first = jnp.where(position >= bound, bound, first)
        first = first - base + MAXDOC
        key_no = lax.broadcasted_iota(jnp.int32, (BLK, WINDOW), 1)
        last = MAXDOC + lax.broadcasted_iota(jnp.int32, (BLK, WINDOW), 0)
        allowed = (key_no >= first) & (key_no <= last)
        for head in range(HEADS):
            columns = pl.ds(head * HEAD_SIZE, HEAD_SIZE)
            scores = lax.dot_general(
                q_ref[rows, columns],
                keys,
                (((1,), (1,)), ((), ())),
                preferred_element_type=jnp.float32,
            )
            scores = jnp.where(allowed, scores * scale, -1e30)
            weights = jnp.exp2(scores - jnp.max(scores, axis=1, keepdims=True))
            total = jnp.sum(weights, axis=1, keepdims=True)
            mix = jnp.dot(
                weights.astype(jnp.bfloat16), values, preferred_element_type=jnp.float32
            )
            attended[rows_of(place), columns] = (mix / total).astype(jnp.bfloat16)

    def project(block, half):
        return jnp.dot(
            att[rows_of(block), :],
            weight[pl.ds(0, 4 * WIDTH), pl.ds(half * WIDTH, WIDTH)],
            preferred_element_type=jnp.float32,
        )

    def route_copy(place, piece, role, target):
        rows = pl.ds(pl.multiple_of(place * BLK + piece * PIECE, PIECE), PIECE)
        return remote(
            (mixed, attended)[role].at[rows],
            midr[role].at[me],
            route_send.at[place, piece],
            mid_recv.at[role],
            {"seq": target},
        )

    my_piece = y * 2 + x // 2

    def my_place(role):
        return lax.rem(x + y, 2) + 2 * core + HALF * role

    def piece_rows(block):
        return pl.ds(pl.multiple_of(block * BLK + my_piece * PIECE, PIECE), PIECE)

    def mid_target(role):
        place = my_place(role)
        if role == 0:
            return out_ref.at[piece_rows(block_at(place))], out_recv.at[place]
        return att.at[piece_rows(place), slot(0)], placed_recv.at[place - HALF]

    def mid_copy(role, target):
        dst, sem = mid_target(role)
        return remote(
            mids.at[role, target], dst, mid_send.at[role, target], sem, {"seq": target}
        )

    def own_mid(role):
        src = (mixed, attended)[role].at[piece_rows(my_place(role))]
        return pltpu.make_async_copy(src, midr[role].at[me], mid_recv.at[role])

    def own_out(role):
        dst, sem = mid_target(role)
        return pltpu.make_async_copy(mids.at[role, me], dst, sem)

    def route(place, role):
        for piece in range(PIECES):
            target = middle_of(place, piece)

            @pl.when(target != me)
            def _():
                route_copy(place, piece, role, target).start()

        @pl.when(place == my_place(role))
        def _():
            own_mid(role).start()

    def reorder(place, role):
        @pl.when(place == my_place(role))
        def _():
            pltpu.make_async_copy(midr[role], midr[role], mid_recv.at[role]).wait()
            block = block_at(place)

            @pl.loop(0, SEQ)
            def _(owner):
                mids[role, owner] = midr[role][inverse_ref[block, owner]]

                @pl.when(owner != me)
                def _():
                    mid_copy(role, owner).start()

                @pl.when(owner == me)
                def _():
                    own_out(role).start()

    def placed_wait(place):
        ref = att.at[rows_of(place), slot(0)]
        pltpu.make_async_copy(ref, ref, placed_recv.at[place - HALF]).wait()

    def own_result(place):
        return pltpu.make_async_copy(
            mixed.at[rows_of(place)], out_ref.at[rows_of(block_at(place))], out_recv.at[place]
        )

    @pl.loop(0, BLOCKS + D_FINAL)
    def _(step):
        @pl.when(step == 0)
        def _():
            own_k.wait()
            own_v.wait()

            @pl.when(j >= 1)
            def _():
                near_kv(0).wait_recv()
                near_kv(1).wait_recv()

        @pl.when(step == 1)
        def _():
            for half in range(2):
                w_first(half).wait_recv()
                for hop in (1, 3, 2):
                    w_second(half, hop).start()

            @pl.when(j < 2)
            def _():
                @pl.loop(1, BLOCKS)
                def _(back):
                    next_kv(0, BLOCKS - 1 - back).start()
                    next_kv(1, BLOCKS - 1 - back).start()

        @pl.when(step == 2)
        def _():
            for half in range(2):
                for hop in (1, 3, 2):
                    w_second(half, hop).wait_recv()
            for hop in (1, 3, 2):
                w_third(0, hop).start()
                for yy in range(4):
                    w_third_piece(hop, yy).start()

        @pl.when(step == 3)
        def _():
            for half in range(2):
                for hop in (1, 3, 2):
                    w_third(half, hop).wait_recv()
                w_fourth(half).start()

        @pl.when((step >= D_FORWARD) & (step < D_FORWARD + BLOCKS))
        def _():
            place = step - D_FORWARD
            far_copy(place).wait_recv()
            forward_copy(place).start()

        @pl.when((step >= HALF) & (step < BLOCKS))
        def _():
            placed_wait(step)
            far_copy(step).start()
            own_copy(step).start()

        @pl.loop(0, 2)
        def _(late):
            place = jnp.where(late == 1, step + HALF - 1, step)
            first_step = late

            @pl.when((step >= first_step) & (step < first_step + HALF))
            def _():
                @pl.when(j >= 2)
                def _():
                    next_kv(0, block_at(place)).wait_recv()
                    next_kv(1, block_at(place)).wait_recv()

                attention(place)

                @pl.when(late == 0)
                def _():
                    rows = rows_of(place)
                    att[rows, slot(0)] = attended[rows, :]
                    far_copy(place).start()
                    own_copy(place).start()

                @pl.when(late == 1)
                def _():
                    route(place, 1)

        reorder(step + 2, 1)

        @pl.when(step == D_PROJ)
        def _():
            for half in range(2):
                own_weight(half).wait()
                w_fourth(half).wait_recv()

        @pl.when((step >= D_PROJ) & (step < D_PROJ + BLOCKS))
        def _():
            place = step - D_PROJ
            rows = rows_of(place)
            own_copy(place).wait_recv()
            forward_copy(place).wait_recv()
            psend[rows, :] = project(place, 1).astype(jnp.bfloat16)
            pair_copy(place).start()
            own_part[rows, :] = project(place, 0)

        @pl.when((step >= D_FINAL) & (step < D_FINAL + BLOCKS))
        def _():
            place = step - D_FINAL
            rows = rows_of(place)
            pair_copy(place).wait_recv()
            mixed[rows, :] = (
                own_part[rows, :] + precv[rows, :].astype(jnp.float32)
            ).astype(jnp.bfloat16)

            @pl.when(place < HALF)
            def _():
                route(place, 0)

            @pl.when(place >= HALF)
            def _():
                own_result(place).start()

        reorder(step - D_MID, 0)

    for block in range(BLOCKS):
        rows = pl.ds(block * BLK, BLK)
        pltpu.make_async_copy(out_ref.at[rows], out_ref.at[rows], out_recv.at[block]).wait()

    @pl.when(j < 3)
    def _():
        near_kv(0).wait_send()
        near_kv(1).wait_send()

    @pl.when(j < 2)
    def _():
        @pl.loop(0, BLOCKS)
        def _(piece):
            next_kv(0, piece).wait_send()
            next_kv(1, piece).wait_send()

    for half in range(2):
        w_first(half).wait_send()
        w_fourth(half).wait_send()
        for hop in (1, 2, 3):
            w_second(half, hop).wait_send()
            w_third(half, hop).wait_send()

    @pl.loop(0, BLOCKS)
    def _(block):
        own_copy(block).wait_send()
        far_copy(block).wait_send()
        forward_copy(block).wait_send()
        pair_copy(block).wait_send()
        for piece in range(PIECES):
            target = middle_of(block, piece)

            @pl.when(target != me)
            def _():
                route_copy(block, piece, 0, target).wait_send()

    @pl.loop(0, SEQ)
    def _(owner):
        @pl.when(owner != me)
        def _():
            mid_copy(0, owner).wait_send()
            mid_copy(1, owner).wait_send()


def body(queries, key_heads, token_value_heads, out_weight, doc_lengths, owner_of):
    index = jnp.arange(SEQ * BLOCKS, dtype=jnp.int32)[None, None, :]
    blocks = jnp.arange(BLOCKS, dtype=jnp.int32)[:, None, None]
    owners = jnp.arange(SEQ, dtype=jnp.int32)[None, :, None]
    inverse = jnp.sum(
        jnp.where(
            (owner_of[None, None, :] == owners) & (index % BLOCKS == blocks), index // BLOCKS, 0
        ),
        axis=2,
    )
    dma = pltpu.SemaphoreType.DMA
    bf16 = jnp.bfloat16
    any_space = pl.BlockSpec(memory_space=pl.ANY)
    smem = pl.BlockSpec(memory_space=pltpu.SMEM)
    vmem = pl.BlockSpec(memory_space=pltpu.VMEM)
    return pl.pallas_call(
        kernel,
        out_shape=jax.ShapeDtypeStruct((ROWS, WIDTH), bf16),
        in_specs=[smem, smem, vmem, any_space, any_space, any_space],
        out_specs=any_space,
        scratch_shapes=[
            pltpu.VMEM((3 * ROWS, HEAD_SIZE), bf16),
            pltpu.VMEM((3 * ROWS, HEAD_SIZE), bf16),
            pltpu.VMEM((W_ROWS, 2 * WIDTH), bf16),
            pltpu.VMEM((ROWS, 4 * WIDTH), bf16),
            pltpu.VMEM((ROWS, WIDTH), bf16),
            pltpu.VMEM((ROWS, WIDTH), bf16),
            pltpu.VMEM((ROWS, WIDTH), jnp.float32),
            pltpu.VMEM((ROWS, WIDTH), bf16),
            pltpu.VMEM((ROWS, WIDTH), bf16),
            pltpu.VMEM((SEQ, PIECE, WIDTH), bf16),
            pltpu.VMEM((SEQ, PIECE, WIDTH), bf16),
            pltpu.VMEM((2, SEQ, PIECE, WIDTH), bf16),
            dma((4,)),
            dma((2, BLOCKS + 1)),
            dma((2, BLOCKS + 1)),
            dma((16,)),
            dma((16,)),
            dma((BLOCKS,)),
            dma((BLOCKS,)),
            dma((BLOCKS,)),
            dma((BLOCKS,)),
            dma((BLOCKS,)),
            dma((BLOCKS,)),
            dma((BLOCKS,)),
            dma((BLOCKS,)),
            dma((BLOCKS, PIECES)),
            dma((2,)),
            dma((2, SEQ)),
            dma((HALF,)),
            dma((BLOCKS,)),
        ],
        compiler_params=pltpu.CompilerParams(
            collective_id=0, has_side_effects=True, vmem_limit_bytes=56 * 1024 * 1024
        ),
        cost_estimate=pl.CostEstimate(
            flops=20_000_000_000, bytes_accessed=12_000_000, transcendentals=11_000_000
        ),
    )(doc_lengths, inverse, queries, key_heads, token_value_heads, out_weight)


def solution(mesh):
    return jax.shard_map(
        body,
        mesh=mesh,
        in_specs=(P("seq", "tp"), P("seq", "tp"), P("seq", "tp"), P("tp", None), P(), P()),
        out_specs=P("seq", "tp"),
        check_vma=False,
    )
```

```python
import functools
import math

import jax
import jax.numpy as jnp
from jax import lax
from jax.experimental import pallas as pl
from jax.experimental.pallas import tpu as pltpu
from jax.sharding import PartitionSpec as P

HEAD_SIZE = 128
BLK = 128
LEN = 4096
MAXDOC = 2048
HEADS = 5
ROWS = 1024
WIDTH = HEADS * HEAD_SIZE
BLOCKS = ROWS // BLK
WINDOW = MAXDOC + BLK
SEQ = 32
TP = 8
PER_SEQ = LEN // ROWS
PIECES = 8
PIECE = BLK // PIECES
W_PIECE = 64
W_ROWS = 4 * WIDTH + 128
MESH = pl.DeviceIdType.MESH

HALF = BLOCKS // 2

D_FORWARD = 2
D_PROJ = 4
D_FINAL = 5
D_MID = 6


def block_at(place):
    late = jnp.where(place == 7, 0, 13 - 2 * place)
    return jnp.where(place < HALF, jnp.where(place == 0, 7, 8 - 2 * place), late)


def pair_of(z):
    return lax.rem(z + jnp.where(lax.rem(z, 2) == 1, 1, TP - 1), TP)


def buddy_of(z):
    return z + 1 - 2 * lax.rem(z, 2)


def far_of(z):
    return lax.rem(z + jnp.where(lax.rem(z, 2) == 1, 3, 5), TP)


def middle_of(place, piece):
    y = piece // 2
    x = 2 * (piece % 2) + lax.rem(y + place, 2)
    return (y * 4 + x) * 2 + lax.rem(place // 2, 2)


def kernel(
    doc_ref,
    owner_ref,
    q_hbm,
    k_hbm,
    v_hbm,
    w_hbm,
    out_ref,
    queries,
    kbuf,
    vbuf,
    probs,
    inverse_vmem,
    inverse_ref,
    weight,
    att,
    psend,
    precv,
    own_part,
    attended,
    mixed,
    midr_low,
    midr_high,
    mids,
    local_sem,
    kv_send,
    kv_recv,
    w_send,
    w_recv,
    own_send,
    own_recv,
    far_send,
    far_recv,
    forward_send,
    forward_recv,
    pair_send,
    pair_recv,
    route_send,
    mid_recv,
    mid_send,
    placed_recv,
    out_recv,
):
    midr = (midr_low, midr_high)
    me = lax.axis_index("seq")
    z = lax.axis_index("tp")
    core = lax.rem(me, 2)
    x = lax.rem(me // 2, 4)
    y = me // 8
    j = lax.rem(me, PER_SEQ)
    pair, buddy, far = pair_of(z), buddy_of(z), far_of(z)
    far_buddy = buddy_of(far)
    scale = math.log2(math.e) / math.sqrt(HEAD_SIZE)

    def remote(src, dst, send, recv, target):
        return pltpu.make_async_remote_copy(
            src_ref=src,
            dst_ref=dst,
            send_sem=send,
            recv_sem=recv,
            device_id=target,
            device_id_type=MESH,
        )

    own_k = pltpu.make_async_copy(k_hbm, kbuf.at[pl.ds(2 * ROWS, ROWS)], local_sem.at[0])
    own_v = pltpu.make_async_copy(v_hbm, vbuf.at[pl.ds(2 * ROWS, ROWS)], local_sem.at[1])
    own_q = pltpu.make_async_copy(q_hbm, queries, local_sem.at[4])
    own_k.start()
    own_q.start()
    own_v.start()

    def own_weight(half):
        column = pl.multiple_of((pair if half else z) * WIDTH, WIDTH)
        return pltpu.make_async_copy(
            w_hbm.at[:, pl.ds(column, WIDTH)],
            weight.at[pl.ds(0, WIDTH), pl.ds(half * WIDTH, WIDTH)],
            local_sem.at[2 + half],
        )

    for half in range(2):
        own_weight(half).start()

    barrier = pltpu.get_barrier_semaphore()

    @pl.loop(1, SEQ)
    def _(step):
        pl.semaphore_signal(
            barrier, inc=1, device_id={"seq": lax.rem(me + step, SEQ)}, device_id_type=MESH
        )

    for target in (pair, buddy, far, far_buddy):
        pl.semaphore_signal(barrier, inc=1, device_id={"tp": target}, device_id_type=MESH)

    block_no = lax.broadcasted_iota(jnp.int32, (8, 128), 0)
    owner_no = lax.broadcasted_iota(jnp.int32, (8, 128), 1)

    def add_index(index, inverse):
        for block in range(BLOCKS):
            here = (block_no == block) & (owner_no == owner_ref[index * BLOCKS + block])
            inverse = jnp.where(here, index, inverse)
        return inverse

    inverse_vmem[...] = lax.fori_loop(0, SEQ, add_index, jnp.zeros((8, 128), jnp.int32))
    to_scalars = pltpu.make_async_copy(inverse_vmem, inverse_ref, local_sem.at[5])
    to_scalars.start()
    pl.semaphore_wait(barrier, SEQ - 1 + 4)

    piece_no = (core * 4 + y) * 4 + x
    group = jnp.minimum(piece_no // 10, 2)
    w_target = jnp.where(group == 0, buddy, jnp.where(group == 1, far, far_buddy))

    def w_rows(yy, xx):
        start = WIDTH + ((core * 4 + yy) * 4 + xx) * W_PIECE
        return pl.ds(pl.multiple_of(start, W_PIECE), W_PIECE)

    def w_half(half):
        return pl.ds(half * WIDTH, WIDTH)

    def w_first(half):
        column = pair_of(w_target) if half else w_target
        src = w_hbm.at[
            pl.ds(pl.multiple_of(lax.rem(piece_no, 10) * W_PIECE, W_PIECE), W_PIECE),
            pl.ds(pl.multiple_of(column * WIDTH, WIDTH), WIDTH),
        ]
        dst = weight.at[w_rows(y, x), w_half(half)]
        return remote(src, dst, w_send.at[half], w_recv.at[half], {"tp": w_target})

    def along_x(hop):
        return {"seq": (y * 4 + lax.rem(x + hop, 4)) * 2 + core}

    def along_y(hop):
        return {"seq": (lax.rem(y + hop, 4) * 4 + x) * 2 + core}

    def w_second(half, hop):
        sem = 2 + half * 3 + hop - 1
        ref = weight.at[w_rows(y, x), w_half(half)]
        target = along_y(hop) if half else along_x(hop)
        return remote(ref, ref, w_send.at[sem], w_recv.at[sem], target)

    four_rows = pl.ds(pl.multiple_of(WIDTH + (core * 4 + y) * 4 * W_PIECE, W_PIECE), 4 * W_PIECE)

    def w_third(half, hop):
        sem = 8 + half * 3 + hop - 1
        ref = weight.at[four_rows, w_half(half)]
        target = along_x(hop) if half else along_y(hop)
        return remote(ref, ref, w_send.at[sem], w_recv.at[sem], target)

    def w_third_piece(hop, yy):
        sem = 11 + hop - 1
        ref = weight.at[w_rows(yy, x), w_half(1)]
        return remote(ref, ref, w_send.at[sem], w_recv.at[sem], along_x(hop))

    def w_fourth(half):
        sem = 14 + half
        rows = pl.ds(pl.multiple_of(WIDTH + core * 16 * W_PIECE, W_PIECE), 16 * W_PIECE)
        ref = weight.at[rows, w_half(half)]
        return remote(ref, ref, w_send.at[sem], w_recv.at[sem], {"seq": me + 1 - 2 * core})

    w_first(0).start()
    w_first(1).start()

    def near_kv(which):
        src, buf = ((k_hbm, kbuf), (v_hbm, vbuf))[which]
        return remote(
            src,
            buf.at[pl.ds(ROWS, ROWS)],
            kv_send.at[which, BLOCKS],
            kv_recv.at[which, BLOCKS],
            {"seq": lax.rem(me + 1, SEQ)},
        )

    def next_kv(which, piece):
        src, buf = ((k_hbm, kbuf), (v_hbm, vbuf))[which]
        rows = pl.ds(pl.multiple_of(piece * BLK, BLK), BLK)
        return remote(
            src.at[rows],
            buf.at[rows],
            kv_send.at[which, piece],
            kv_recv.at[which, piece],
            {"seq": lax.rem(me + 2, SEQ)},
        )

    for which in range(2):

        @pl.when(j < 3)
        def _():
            near_kv(which).start()

        @pl.when(j < 2)
        def _():
            next_kv(which, BLOCKS - 1).start()

    @pl.when(j < 2)
    def _():
        kbuf[pl.ds(0, ROWS), :] = jnp.zeros((ROWS, HEAD_SIZE), kbuf.dtype)
        vbuf[pl.ds(0, ROWS), :] = jnp.zeros((ROWS, HEAD_SIZE), vbuf.dtype)

    @pl.when(j < 1)
    def _():
        kbuf[pl.ds(ROWS, ROWS), :] = jnp.zeros((ROWS, HEAD_SIZE), kbuf.dtype)
        vbuf[pl.ds(ROWS, ROWS), :] = jnp.zeros((ROWS, HEAD_SIZE), vbuf.dtype)

    def rows_of(block):
        return pl.ds(pl.multiple_of(block * BLK, BLK), BLK)

    def slot(no):
        return pl.ds(no * WIDTH, WIDTH)

    def span(place, part):
        if part is None:
            return rows_of(place), place
        return pl.ds((BLOCKS - 1) * BLK + part * (BLK // 2), BLK // 2), BLOCKS - 1 + part

    def own_copy(block):
        rows = rows_of(block)
        return remote(
            att.at[rows, slot(0)],
            att.at[rows, slot(1)],
            own_send.at[block],
            own_recv.at[block],
            {"tp": buddy},
        )

    def far_copy(place, part=None):
        rows, sem = span(place, part)
        return remote(
            att.at[rows, slot(0)],
            att.at[rows, slot(2)],
            far_send.at[sem],
            far_recv.at[sem],
            {"tp": far},
        )

    def forward_copy(place, part=None):
        rows, sem = span(place, part)
        return remote(
            att.at[rows, slot(2)],
            att.at[rows, slot(3)],
            forward_send.at[sem],
            forward_recv.at[sem],
            {"tp": buddy},
        )

    def pair_copy(place, part=None):
        rows, sem = span(place, part)
        return remote(
            psend.at[rows], precv.at[rows], pair_send.at[sem], pair_recv.at[sem], {"tp": pair}
        )

    def wait_kv(step, block, which):
        @pl.when(step == 0)
        def _():
            (own_k, own_v)[which].wait()

        @pl.when((step == 0) & (j >= 1))
        def _():
            near_kv(which).wait_recv()

        @pl.when(j >= 2)
        def _():
            next_kv(which, block).wait_recv()

    def attention(step, place):
        block = block_at(place)
        rows = rows_of(block)
        window = pl.ds(pl.multiple_of(block * BLK, BLK), WINDOW)
        wait_kv(step, block, 0)
        keys = kbuf[window, :]
        base = j * ROWS + block * BLK
        position = base + lax.broadcasted_iota(jnp.int32, (BLK, 1), 0)
        bound = jnp.int32(0)
        first = jnp.zeros((BLK, 1), jnp.int32)
        for doc in range(doc_ref.shape[1]):
            bound = bound + doc_ref[me // PER_SEQ, doc]
            first = jnp.where(position >= bound, bound, first)
        first = first - base + MAXDOC
        key_no = lax.broadcasted_iota(jnp.int32, (BLK, WINDOW), 1)
        last = MAXDOC + lax.broadcasted_iota(jnp.int32, (BLK, WINDOW), 0)
        allowed = (key_no >= first) & (key_no <= last)
        totals = []
        for head in range(HEADS):
            columns = pl.ds(head * HEAD_SIZE, HEAD_SIZE)
            scores = lax.dot_general(
                queries[rows, columns],
                keys,
                (((1,), (1,)), ((), ())),
                preferred_element_type=jnp.float32,
            )
            scores = jnp.where(allowed, scores * scale, -1e30)
            weights = jnp.exp2(scores - jnp.max(scores, axis=1, keepdims=True))
            totals.append(jnp.sum(weights, axis=1, keepdims=True))
            probs[pl.ds(head * BLK, BLK), :] = weights.astype(jnp.bfloat16)
        wait_kv(step, block, 1)
        mix = jnp.dot(probs[...], vbuf[window, :], preferred_element_type=jnp.float32)
        for head in range(HEADS):
            part = mix[head * BLK : (head + 1) * BLK] / totals[head]
            columns = pl.ds(head * HEAD_SIZE, HEAD_SIZE)
            attended[rows_of(place), columns] = part.astype(jnp.bfloat16)

    def project(rows, half):
        return jnp.dot(
            att[rows, :],
            weight[pl.ds(0, 4 * WIDTH), pl.ds(half * WIDTH, WIDTH)],
            preferred_element_type=jnp.float32,
        )

    def route_copy(place, piece, role, target):
        rows = pl.ds(pl.multiple_of(place * BLK + piece * PIECE, PIECE), PIECE)
        return remote(
            (mixed, attended)[role].at[rows],
            midr[role].at[me],
            route_send.at[place, piece],
            mid_recv.at[role],
            {"seq": target},
        )

    my_piece = y * 2 + x // 2

    def my_place(role):
        return lax.rem(x + y, 2) + 2 * core + HALF * role

    def piece_rows(block):
        return pl.ds(pl.multiple_of(block * BLK + my_piece * PIECE, PIECE), PIECE)

    def mid_target(role):
        place = my_place(role)
        if role == 0:
            return out_ref.at[piece_rows(block_at(place))], out_recv.at[place]
        return att.at[piece_rows(place), slot(0)], placed_recv.at[place - HALF]

    def mid_copy(role, target):
        dst, sem = mid_target(role)
        return remote(
            mids.at[role, target], dst, mid_send.at[role, target], sem, {"seq": target}
        )

    def own_mid(role):
        src = (mixed, attended)[role].at[piece_rows(my_place(role))]
        return pltpu.make_async_copy(src, midr[role].at[me], mid_recv.at[role])

    def own_out(role):
        dst, sem = mid_target(role)
        return pltpu.make_async_copy(mids.at[role, me], dst, sem)

    def route(place, role):
        for piece in range(PIECES):
            target = middle_of(place, piece)

            @pl.when(target != me)
            def _():
                route_copy(place, piece, role, target).start()

        @pl.when(place == my_place(role))
        def _():
            own_mid(role).start()

    def reorder(place, role):
        @pl.when(place == my_place(role))
        def _():
            pltpu.make_async_copy(midr[role], midr[role], mid_recv.at[role]).wait()
            block = block_at(place)

            @pl.loop(0, SEQ)
            def _(owner):
                mids[role, owner] = midr[role][inverse_ref[block, owner]]

                @pl.when(owner != me)
                def _():
                    mid_copy(role, owner).start()

                @pl.when(owner == me)
                def _():
                    own_out(role).start()

    def placed_wait(place):
        ref = att.at[rows_of(place), slot(0)]
        pltpu.make_async_copy(ref, ref, placed_recv.at[place - HALF]).wait()

    def own_result(place, part=None):
        rows = span(place, part)[0]
        if part is None:
            out_rows = rows_of(block_at(place))
        else:
            out_rows = pl.ds(part * (BLK // 2), BLK // 2)
        return pltpu.make_async_copy(
            mixed.at[rows], out_ref.at[out_rows], out_recv.at[place]
        )

    def parts_of(place):
        return [
            lambda f: pl.when(place < BLOCKS - 1)(lambda: f(None)),
            lambda f: pl.when(place == BLOCKS - 1)(lambda: (f(0), f(1))[0]),
        ]

    @pl.loop(0, BLOCKS + D_FINAL)
    def _(step):
        @pl.when(step == 0)
        def _():
            own_q.wait()
            to_scalars.wait()

        @pl.when(step == 1)
        def _():
            for half in range(2):
                w_first(half).wait_recv()
                for hop in (1, 3, 2):
                    w_second(half, hop).start()

            @pl.when(j < 2)
            def _():
                @pl.loop(1, BLOCKS)
                def _(back):
                    next_kv(0, BLOCKS - 1 - back).start()
                    next_kv(1, BLOCKS - 1 - back).start()

        @pl.when(step == 2)
        def _():
            for half in range(2):
                for hop in (1, 3, 2):
                    w_second(half, hop).wait_recv()
            for hop in (1, 3, 2):
                w_third(0, hop).start()
                for yy in range(4):
                    w_third_piece(hop, yy).start()

        @pl.when(step == 3)
        def _():
            for half in range(2):
                for hop in (1, 3, 2):
                    w_third(half, hop).wait_recv()
                w_fourth(half).start()

        @pl.when((step >= D_FORWARD) & (step < D_FORWARD + BLOCKS))
        def _():
            place = step - D_FORWARD
            for part in parts_of(place):

                @part
                def _(number):
                    far_copy(place, number).wait_recv()
                    forward_copy(place, number).start()

        @pl.when((step >= HALF) & (step < BLOCKS))
        def _():
            placed_wait(step)
            for part in parts_of(step):

                @part
                def _(number):
                    far_copy(step, number).start()

            own_copy(step).start()

        @pl.loop(0, 2)
        def _(late):
            place = jnp.where(late == 1, step + HALF - 1, step)
            first_step = late

            @pl.when((step >= first_step) & (step < first_step + HALF))
            def _():
                attention(step, place)

                @pl.when(late == 0)
                def _():
                    rows = rows_of(place)
                    att[rows, slot(0)] = attended[rows, :]
                    far_copy(place).start()
                    own_copy(place).start()

                @pl.when(late == 1)
                def _():
                    route(place, 1)

        reorder(step + 2, 1)

        @pl.when(step == D_PROJ)
        def _():
            for half in range(2):
                own_weight(half).wait()
                w_fourth(half).wait_recv()

        @pl.when((step >= D_PROJ) & (step < D_PROJ + BLOCKS))
        def _():
            place = step - D_PROJ
            own_copy(place).wait_recv()
            for part in parts_of(place):

                @part
                def _(number):
                    rows = span(place, number)[0]
                    forward_copy(place, number).wait_recv()
                    psend[rows, :] = project(rows, 1).astype(jnp.bfloat16)
                    pair_copy(place, number).start()

            rows = rows_of(place)
            own_part[rows, :] = project(rows, 0)

        @pl.when((step >= D_FINAL) & (step < D_FINAL + BLOCKS))
        def _():
            place = step - D_FINAL
            for part in parts_of(place):

                @part
                def _(number):
                    rows = span(place, number)[0]
                    pair_copy(place, number).wait_recv()
                    mixed[rows, :] = (
                        own_part[rows, :] + precv[rows, :].astype(jnp.float32)
                    ).astype(jnp.bfloat16)

                    @pl.when(place >= HALF)
                    def _():
                        own_result(place, number).start()

            @pl.when(place < HALF)
            def _():
                route(place, 0)

        reorder(step - D_MID, 0)

    for block in range(BLOCKS):
        rows = pl.ds(block * BLK, BLK)
        pltpu.make_async_copy(out_ref.at[rows], out_ref.at[rows], out_recv.at[block]).wait()

    @pl.when(j < 3)
    def _():
        near_kv(0).wait_send()
        near_kv(1).wait_send()

    @pl.when(j < 2)
    def _():
        @pl.loop(0, BLOCKS)
        def _(piece):
            next_kv(0, piece).wait_send()
            next_kv(1, piece).wait_send()

    for half in range(2):
        w_first(half).wait_send()
        w_fourth(half).wait_send()
        for hop in (1, 2, 3):
            w_second(half, hop).wait_send()
            w_third(half, hop).wait_send()

    @pl.loop(0, BLOCKS)
    def _(block):
        own_copy(block).wait_send()
        for part in parts_of(block):

            @part
            def _(number):
                far_copy(block, number).wait_send()
                forward_copy(block, number).wait_send()
                pair_copy(block, number).wait_send()

        for piece in range(PIECES):
            target = middle_of(block, piece)

            @pl.when(target != me)
            def _():
                route_copy(block, piece, 0, target).wait_send()

    @pl.loop(0, SEQ)
    def _(owner):
        @pl.when(owner != me)
        def _():
            mid_copy(0, owner).wait_send()
            mid_copy(1, owner).wait_send()


def body(queries, key_heads, token_value_heads, out_weight, doc_lengths, owner_of):
    dma = pltpu.SemaphoreType.DMA
    bf16 = jnp.bfloat16
    any_space = pl.BlockSpec(memory_space=pl.ANY)
    smem = pl.BlockSpec(memory_space=pltpu.SMEM)
    return pl.pallas_call(
        kernel,
        out_shape=jax.ShapeDtypeStruct((ROWS, WIDTH), bf16),
        in_specs=[smem, smem] + [any_space] * 4,
        out_specs=any_space,
        scratch_shapes=[
            pltpu.VMEM((ROWS, WIDTH), bf16),
            pltpu.VMEM((3 * ROWS, HEAD_SIZE), bf16),
            pltpu.VMEM((3 * ROWS, HEAD_SIZE), bf16),
            pltpu.VMEM((HEADS * BLK, WINDOW), bf16),
            pltpu.VMEM((8, 128), jnp.int32),
            pltpu.SMEM((8, 128), jnp.int32),
            pltpu.VMEM((W_ROWS, 2 * WIDTH), bf16),
            pltpu.VMEM((ROWS, 4 * WIDTH), bf16),
            pltpu.VMEM((ROWS, WIDTH), bf16),
            pltpu.VMEM((ROWS, WIDTH), bf16),
            pltpu.VMEM((ROWS, WIDTH), jnp.float32),
            pltpu.VMEM((ROWS, WIDTH), bf16),
            pltpu.VMEM((ROWS, WIDTH), bf16),
            pltpu.VMEM((SEQ, PIECE, WIDTH), bf16),
            pltpu.VMEM((SEQ, PIECE, WIDTH), bf16),
            pltpu.VMEM((2, SEQ, PIECE, WIDTH), bf16),
            dma((6,)),
            dma((2, BLOCKS + 1)),
            dma((2, BLOCKS + 1)),
            dma((16,)),
            dma((16,)),
            dma((BLOCKS,)),
            dma((BLOCKS,)),
            dma((BLOCKS + 1,)),
            dma((BLOCKS + 1,)),
            dma((BLOCKS + 1,)),
            dma((BLOCKS + 1,)),
            dma((BLOCKS + 1,)),
            dma((BLOCKS + 1,)),
            dma((BLOCKS, PIECES)),
            dma((2,)),
            dma((2, SEQ)),
            dma((HALF,)),
            dma((BLOCKS,)),
        ],
        compiler_params=pltpu.CompilerParams(
            collective_id=0, has_side_effects=True, vmem_limit_bytes=56 * 1024 * 1024
        ),
        cost_estimate=pl.CostEstimate(
            flops=20_000_000_000, bytes_accessed=12_000_000, transcendentals=11_000_000
        ),
    )(doc_lengths, owner_of, queries, key_heads, token_value_heads, out_weight)


def solution(mesh):
    return jax.shard_map(
        body,
        mesh=mesh,
        in_specs=(P("seq", "tp"), P("seq", "tp"), P("seq", "tp"), P("tp", None), P(), P()),
        out_specs=P("seq", "tp"),
        check_vma=False,
    )
```

```python
import functools
import math

import jax
import jax.numpy as jnp
from jax import lax
from jax.experimental import pallas as pl
from jax.experimental.pallas import tpu as pltpu
from jax.sharding import PartitionSpec as P

HEAD_SIZE = 128
BLK = 128
LEN = 4096
MAXDOC = 2048
HEADS = 5
ROWS = 1024
WIDTH = HEADS * HEAD_SIZE
BLOCKS = ROWS // BLK
WINDOW = MAXDOC + BLK
SEQ = 32
TP = 8
PER_SEQ = LEN // ROWS
PIECES = 8
PIECE = BLK // PIECES
W_PIECE = 64
W_ROWS = 4 * WIDTH + 128
MESH = pl.DeviceIdType.MESH

HALF = BLOCKS // 2

D_FORWARD = 1
D_PROJ = 3
D_FINAL = 4
D_MID = 5


def block_at(place):
    late = jnp.where(place == 7, 0, 13 - 2 * place)
    return jnp.where(place < HALF, jnp.where(place == 0, 7, 8 - 2 * place), late)


def pair_of(z):
    return lax.rem(z + jnp.where(lax.rem(z, 2) == 1, 1, TP - 1), TP)


def buddy_of(z):
    return z + 1 - 2 * lax.rem(z, 2)


def far_of(z):
    return lax.rem(z + jnp.where(lax.rem(z, 2) == 1, 3, 5), TP)


def middle_of(place, piece):
    y = piece // 2
    x = 2 * (piece % 2) + lax.rem(y + place, 2)
    return (y * 4 + x) * 2 + lax.rem(place // 2, 2)


def kernel(
    doc_ref,
    owner_ref,
    q_hbm,
    k_hbm,
    v_hbm,
    w_hbm,
    out_ref,
    queries,
    kbuf,
    vbuf,
    probs,
    inverse_vmem,
    inverse_ref,
    weight,
    att,
    psend,
    precv,
    own_part,
    attended,
    mixed,
    midr_low,
    midr_high,
    mids,
    local_sem,
    kv_send,
    kv_recv,
    w_send,
    w_recv,
    own_send,
    own_recv,
    far_send,
    far_recv,
    forward_send,
    forward_recv,
    pair_send,
    pair_recv,
    route_send,
    mid_recv,
    mid_send,
    placed_recv,
    out_recv,
):
    midr = (midr_low, midr_high)
    me = lax.axis_index("seq")
    z = lax.axis_index("tp")
    core = lax.rem(me, 2)
    x = lax.rem(me // 2, 4)
    y = me // 8
    j = lax.rem(me, PER_SEQ)
    pair, buddy, far = pair_of(z), buddy_of(z), far_of(z)
    far_buddy = buddy_of(far)
    scale = math.log2(math.e) / math.sqrt(HEAD_SIZE)

    def remote(src, dst, send, recv, target):
        return pltpu.make_async_remote_copy(
            src_ref=src,
            dst_ref=dst,
            send_sem=send,
            recv_sem=recv,
            device_id=target,
            device_id_type=MESH,
        )

    own_k = pltpu.make_async_copy(k_hbm, kbuf.at[pl.ds(2 * ROWS, ROWS)], local_sem.at[0])
    own_v = pltpu.make_async_copy(v_hbm, vbuf.at[pl.ds(2 * ROWS, ROWS)], local_sem.at[1])
    own_q = pltpu.make_async_copy(q_hbm, queries, local_sem.at[4])
    own_k.start()
    own_q.start()
    own_v.start()

    def own_weight(half):
        column = pl.multiple_of((pair if half else z) * WIDTH, WIDTH)
        return pltpu.make_async_copy(
            w_hbm.at[:, pl.ds(column, WIDTH)],
            weight.at[pl.ds(0, WIDTH), pl.ds(half * WIDTH, WIDTH)],
            local_sem.at[2 + half],
        )

    for half in range(2):
        own_weight(half).start()

    barrier = pltpu.get_barrier_semaphore()

    @pl.loop(1, SEQ)
    def _(step):
        pl.semaphore_signal(
            barrier, inc=1, device_id={"seq": lax.rem(me + step, SEQ)}, device_id_type=MESH
        )

    for target in (pair, buddy, far, far_buddy):
        pl.semaphore_signal(barrier, inc=1, device_id={"tp": target}, device_id_type=MESH)

    block_no = lax.broadcasted_iota(jnp.int32, (8, 128), 0)
    owner_no = lax.broadcasted_iota(jnp.int32, (8, 128), 1)

    def add_index(index, inverse):
        for block in range(BLOCKS):
            here = (block_no == block) & (owner_no == owner_ref[index * BLOCKS + block])
            inverse = jnp.where(here, index, inverse)
        return inverse

    inverse_vmem[...] = lax.fori_loop(0, SEQ, add_index, jnp.zeros((8, 128), jnp.int32))
    to_scalars = pltpu.make_async_copy(inverse_vmem, inverse_ref, local_sem.at[5])
    to_scalars.start()
    pl.semaphore_wait(barrier, SEQ - 1 + 4)

    piece_no = (core * 4 + y) * 4 + x
    group = jnp.minimum(piece_no // 10, 2)
    w_target = jnp.where(group == 0, buddy, jnp.where(group == 1, far, far_buddy))

    def w_rows(yy, xx):
        start = WIDTH + ((core * 4 + yy) * 4 + xx) * W_PIECE
        return pl.ds(pl.multiple_of(start, W_PIECE), W_PIECE)

    def w_half(half):
        return pl.ds(half * WIDTH, WIDTH)

    def w_first(half):
        column = pair_of(w_target) if half else w_target
        src = w_hbm.at[
            pl.ds(pl.multiple_of(lax.rem(piece_no, 10) * W_PIECE, W_PIECE), W_PIECE),
            pl.ds(pl.multiple_of(column * WIDTH, WIDTH), WIDTH),
        ]
        dst = weight.at[w_rows(y, x), w_half(half)]
        return remote(src, dst, w_send.at[half], w_recv.at[half], {"tp": w_target})

    def along_x(hop):
        return {"seq": (y * 4 + lax.rem(x + hop, 4)) * 2 + core}

    def along_y(hop):
        return {"seq": (lax.rem(y + hop, 4) * 4 + x) * 2 + core}

    def w_second(half, hop):
        sem = 2 + half * 3 + hop - 1
        ref = weight.at[w_rows(y, x), w_half(half)]
        target = along_y(hop) if half else along_x(hop)
        return remote(ref, ref, w_send.at[sem], w_recv.at[sem], target)

    four_rows = pl.ds(pl.multiple_of(WIDTH + (core * 4 + y) * 4 * W_PIECE, W_PIECE), 4 * W_PIECE)

    def w_third(half, hop):
        sem = 8 + half * 3 + hop - 1
        ref = weight.at[four_rows, w_half(half)]
        target = along_x(hop) if half else along_y(hop)
        return remote(ref, ref, w_send.at[sem], w_recv.at[sem], target)

    def w_third_piece(hop, yy):
        sem = 11 + hop - 1
        ref = weight.at[w_rows(yy, x), w_half(1)]
        return remote(ref, ref, w_send.at[sem], w_recv.at[sem], along_x(hop))

    def w_fourth(half):
        sem = 14 + half
        rows = pl.ds(pl.multiple_of(WIDTH + core * 16 * W_PIECE, W_PIECE), 16 * W_PIECE)
        ref = weight.at[rows, w_half(half)]
        return remote(ref, ref, w_send.at[sem], w_recv.at[sem], {"seq": me + 1 - 2 * core})

    w_first(1).start()
    w_first(0).start()

    def near_kv(which):
        src, buf = ((k_hbm, kbuf), (v_hbm, vbuf))[which]
        return remote(
            src,
            buf.at[pl.ds(ROWS, ROWS)],
            kv_send.at[which, BLOCKS],
            kv_recv.at[which, BLOCKS],
            {"seq": lax.rem(me + 1, SEQ)},
        )

    def next_kv(which, piece):
        src, buf = ((k_hbm, kbuf), (v_hbm, vbuf))[which]
        rows = pl.ds(pl.multiple_of(piece * BLK, BLK), BLK)
        return remote(
            src.at[rows],
            buf.at[rows],
            kv_send.at[which, piece],
            kv_recv.at[which, piece],
            {"seq": lax.rem(me + 2, SEQ)},
        )

    for which in range(2):

        @pl.when(j < 3)
        def _():
            near_kv(which).start()

        @pl.when(j < 2)
        def _():
            next_kv(which, BLOCKS - 1).start()

    @pl.when(j < 2)
    def _():
        kbuf[pl.ds(0, ROWS), :] = jnp.zeros((ROWS, HEAD_SIZE), kbuf.dtype)
        vbuf[pl.ds(0, ROWS), :] = jnp.zeros((ROWS, HEAD_SIZE), vbuf.dtype)

    @pl.when(j < 1)
    def _():
        kbuf[pl.ds(ROWS, ROWS), :] = jnp.zeros((ROWS, HEAD_SIZE), kbuf.dtype)
        vbuf[pl.ds(ROWS, ROWS), :] = jnp.zeros((ROWS, HEAD_SIZE), vbuf.dtype)

    def rows_of(block):
        return pl.ds(pl.multiple_of(block * BLK, BLK), BLK)

    def slot(no):
        return pl.ds(no * WIDTH, WIDTH)

    def span(place, part):
        if part is None:
            return rows_of(place), place
        return pl.ds((BLOCKS - 1) * BLK + part * (BLK // 2), BLK // 2), BLOCKS - 1 + part

    def own_copy(block):
        rows = rows_of(block)
        return remote(
            att.at[rows, slot(0)],
            att.at[rows, slot(1)],
            own_send.at[block],
            own_recv.at[block],
            {"tp": buddy},
        )

    def far_copy(place, part=None):
        rows, sem = span(place, part)
        return remote(
            att.at[rows, slot(0)],
            att.at[rows, slot(2)],
            far_send.at[sem],
            far_recv.at[sem],
            {"tp": far},
        )

    def forward_copy(place, part=None):
        rows, sem = span(place, part)
        return remote(
            att.at[rows, slot(2)],
            att.at[rows, slot(3)],
            forward_send.at[sem],
            forward_recv.at[sem],
            {"tp": buddy},
        )

    def pair_copy(place, part=None):
        rows, sem = span(place, part)
        return remote(
            psend.at[rows], precv.at[rows], pair_send.at[sem], pair_recv.at[sem], {"tp": pair}
        )

    def wait_kv(step, block, which):
        @pl.when(step == 0)
        def _():
            (own_k, own_v)[which].wait()

        @pl.when((step == 0) & (j >= 1))
        def _():
            near_kv(which).wait_recv()

        @pl.when(j >= 2)
        def _():
            next_kv(which, block).wait_recv()

    def attention(step, place):
        block = block_at(place)
        rows = rows_of(block)
        window = pl.ds(pl.multiple_of(block * BLK, BLK), WINDOW)
        wait_kv(step, block, 0)
        keys = kbuf[window, :]
        base = j * ROWS + block * BLK
        position = base + lax.broadcasted_iota(jnp.int32, (BLK, 1), 0)
        bound = jnp.int32(0)
        first = jnp.zeros((BLK, 1), jnp.int32)
        for doc in range(doc_ref.shape[1]):
            bound = bound + doc_ref[me // PER_SEQ, doc]
            first = jnp.where(position >= bound, bound, first)
        first = first - base + MAXDOC
        key_no = lax.broadcasted_iota(jnp.int32, (BLK, WINDOW), 1)
        last = MAXDOC + lax.broadcasted_iota(jnp.int32, (BLK, WINDOW), 0)
        allowed = (key_no >= first) & (key_no <= last)
        totals = []
        for head in range(HEADS):
            columns = pl.ds(head * HEAD_SIZE, HEAD_SIZE)
            scores = lax.dot_general(
                queries[rows, columns],
                keys,
                (((1,), (1,)), ((), ())),
                preferred_element_type=jnp.float32,
            )
            scores = jnp.where(allowed, scores * scale, -1e30)
            weights = jnp.exp2(scores - jnp.max(scores, axis=1, keepdims=True))
            totals.append(jnp.sum(weights, axis=1, keepdims=True))
            probs[pl.ds(head * BLK, BLK), :] = weights.astype(jnp.bfloat16)
        wait_kv(step, block, 1)
        mix = jnp.dot(probs[...], vbuf[window, :], preferred_element_type=jnp.float32)
        for head in range(HEADS):
            part = mix[head * BLK : (head + 1) * BLK] / totals[head]
            columns = pl.ds(head * HEAD_SIZE, HEAD_SIZE)
            attended[rows_of(place), columns] = part.astype(jnp.bfloat16)

    def project(rows, half):
        return jnp.dot(
            att[rows, :],
            weight[pl.ds(0, 4 * WIDTH), pl.ds(half * WIDTH, WIDTH)],
            preferred_element_type=jnp.float32,
        )

    def route_copy(place, piece, role, target):
        rows = pl.ds(pl.multiple_of(place * BLK + piece * PIECE, PIECE), PIECE)
        return remote(
            (mixed, attended)[role].at[rows],
            midr[role].at[me],
            route_send.at[place, piece],
            mid_recv.at[role],
            {"seq": target},
        )

    my_piece = y * 2 + x // 2

    def my_place(role):
        return lax.rem(x + y, 2) + 2 * core + HALF * role

    def piece_rows(block):
        return pl.ds(pl.multiple_of(block * BLK + my_piece * PIECE, PIECE), PIECE)

    def mid_target(role):
        place = my_place(role)
        if role == 0:
            return out_ref.at[piece_rows(block_at(place))], out_recv.at[place]
        return att.at[piece_rows(place), slot(0)], placed_recv.at[place - HALF]

    def mid_copy(role, target):
        dst, sem = mid_target(role)
        return remote(
            mids.at[role, target], dst, mid_send.at[role, target], sem, {"seq": target}
        )

    def own_mid(role):
        src = (mixed, attended)[role].at[piece_rows(my_place(role))]
        return pltpu.make_async_copy(src, midr[role].at[me], mid_recv.at[role])

    def own_out(role):
        dst, sem = mid_target(role)
        return pltpu.make_async_copy(mids.at[role, me], dst, sem)

    def route(place, role):
        for piece in range(PIECES):
            target = middle_of(place, piece)

            @pl.when(target != me)
            def _():
                route_copy(place, piece, role, target).start()

        @pl.when(place == my_place(role))
        def _():
            own_mid(role).start()

    def reorder(place, role):
        @pl.when(place == my_place(role))
        def _():
            pltpu.make_async_copy(midr[role], midr[role], mid_recv.at[role]).wait()
            block = block_at(place)

            @pl.loop(0, SEQ)
            def _(owner):
                mids[role, owner] = midr[role][inverse_ref[block, owner]]

                @pl.when(owner != me)
                def _():
                    mid_copy(role, owner).start()

                @pl.when(owner == me)
                def _():
                    own_out(role).start()

    def placed_wait(place):
        ref = att.at[rows_of(place), slot(0)]
        pltpu.make_async_copy(ref, ref, placed_recv.at[place - HALF]).wait()

    def own_result(place, part=None):
        rows = span(place, part)[0]
        if part is None:
            out_rows = rows_of(block_at(place))
        else:
            out_rows = pl.ds(part * (BLK // 2), BLK // 2)
        return pltpu.make_async_copy(
            mixed.at[rows], out_ref.at[out_rows], out_recv.at[place]
        )

    def parts_of(place):
        return [
            lambda f: pl.when(place < BLOCKS - 1)(lambda: f(None)),
            lambda f: pl.when(place == BLOCKS - 1)(lambda: (f(0), f(1))[0]),
        ]

    @pl.loop(0, BLOCKS + D_FINAL)
    def _(step):
        @pl.when(step == 0)
        def _():
            own_q.wait()
            to_scalars.wait()

        @pl.when(step == 1)
        def _():
            for half in (1, 0):
                w_first(half).wait_recv()
                for hop in (1, 3, 2):
                    w_second(half, hop).start()

            @pl.when(j < 2)
            def _():
                @pl.loop(1, BLOCKS)
                def _(back):
                    next_kv(0, BLOCKS - 1 - back).start()
                    next_kv(1, BLOCKS - 1 - back).start()

        @pl.when(step == 2)
        def _():
            for hop in (1, 3, 2):
                w_second(1, hop).wait_recv()
            for hop in (1, 3, 2):
                for yy in range(4):
                    w_third_piece(hop, yy).start()
            for hop in (1, 3, 2):
                w_second(0, hop).wait_recv()
            for hop in (1, 3, 2):
                w_third(0, hop).start()

        @pl.when((step >= HALF) & (step < BLOCKS))
        def _():
            placed_wait(step)
            for part in parts_of(step):

                @part
                def _(number):
                    far_copy(step, number).start()

            own_copy(step).start()

        @pl.loop(0, 2)
        def _(late):
            place = jnp.where(late == 1, step + HALF - 1, step)
            first_step = late

            @pl.when((step >= first_step) & (step < first_step + HALF))
            def _():
                attention(step, place)

                @pl.when(late == 0)
                def _():
                    rows = rows_of(place)
                    att[rows, slot(0)] = attended[rows, :]
                    far_copy(place).start()
                    own_copy(place).start()

                @pl.when(late == 1)
                def _():
                    route(place, 1)

        @pl.when((step >= D_FORWARD) & (step < D_FORWARD + BLOCKS))
        def _():
            place = step - D_FORWARD
            for part in parts_of(place):

                @part
                def _(number):
                    far_copy(place, number).wait_recv()
                    forward_copy(place, number).start()

        @pl.when(step == 3)
        def _():
            for half in (1, 0):
                for hop in (1, 3, 2):
                    w_third(half, hop).wait_recv()
                w_fourth(half).start()

        reorder(step + 2, 1)

        @pl.when(step == D_PROJ)
        def _():
            own_weight(1).wait()
            w_fourth(1).wait_recv()

        @pl.when((step >= D_PROJ) & (step < D_PROJ + BLOCKS))
        def _():
            place = step - D_PROJ
            own_copy(place).wait_recv()
            for part in parts_of(place):

                @part
                def _(number):
                    rows = span(place, number)[0]
                    forward_copy(place, number).wait_recv()
                    psend[rows, :] = project(rows, 1).astype(jnp.bfloat16)
                    pair_copy(place, number).start()

            @pl.when(place == 0)
            def _():
                own_weight(0).wait()
                w_fourth(0).wait_recv()

            rows = rows_of(place)
            own_part[rows, :] = project(rows, 0)

        @pl.when((step >= D_FINAL) & (step < D_FINAL + BLOCKS))
        def _():
            place = step - D_FINAL
            for part in parts_of(place):

                @part
                def _(number):
                    rows = span(place, number)[0]
                    pair_copy(place, number).wait_recv()
                    mixed[rows, :] = (
                        own_part[rows, :] + precv[rows, :].astype(jnp.float32)
                    ).astype(jnp.bfloat16)

                    @pl.when(place >= HALF)
                    def _():
                        own_result(place, number).start()

            @pl.when(place < HALF)
            def _():
                route(place, 0)

        reorder(step - D_MID, 0)

    for block in range(BLOCKS):
        rows = pl.ds(block * BLK, BLK)
        pltpu.make_async_copy(out_ref.at[rows], out_ref.at[rows], out_recv.at[block]).wait()

    @pl.when(j < 3)
    def _():
        near_kv(0).wait_send()
        near_kv(1).wait_send()

    @pl.when(j < 2)
    def _():
        @pl.loop(0, BLOCKS)
        def _(piece):
            next_kv(0, piece).wait_send()
            next_kv(1, piece).wait_send()

    for half in range(2):
        w_first(half).wait_send()
        w_fourth(half).wait_send()
        for hop in (1, 2, 3):
            w_second(half, hop).wait_send()
            w_third(half, hop).wait_send()

    @pl.loop(0, BLOCKS)
    def _(block):
        own_copy(block).wait_send()
        for part in parts_of(block):

            @part
            def _(number):
                far_copy(block, number).wait_send()
                forward_copy(block, number).wait_send()
                pair_copy(block, number).wait_send()

        for piece in range(PIECES):
            target = middle_of(block, piece)

            @pl.when(target != me)
            def _():
                route_copy(block, piece, 0, target).wait_send()

    @pl.loop(0, SEQ)
    def _(owner):
        @pl.when(owner != me)
        def _():
            mid_copy(0, owner).wait_send()
            mid_copy(1, owner).wait_send()


def body(queries, key_heads, token_value_heads, out_weight, doc_lengths, owner_of):
    dma = pltpu.SemaphoreType.DMA
    bf16 = jnp.bfloat16
    any_space = pl.BlockSpec(memory_space=pl.ANY)
    smem = pl.BlockSpec(memory_space=pltpu.SMEM)
    return pl.pallas_call(
        kernel,
        out_shape=jax.ShapeDtypeStruct((ROWS, WIDTH), bf16),
        in_specs=[smem, smem] + [any_space] * 4,
        out_specs=any_space,
        scratch_shapes=[
            pltpu.VMEM((ROWS, WIDTH), bf16),
            pltpu.VMEM((3 * ROWS, HEAD_SIZE), bf16),
            pltpu.VMEM((3 * ROWS, HEAD_SIZE), bf16),
            pltpu.VMEM((HEADS * BLK, WINDOW), bf16),
            pltpu.VMEM((8, 128), jnp.int32),
            pltpu.SMEM((8, 128), jnp.int32),
            pltpu.VMEM((W_ROWS, 2 * WIDTH), bf16),
            pltpu.VMEM((ROWS, 4 * WIDTH), bf16),
            pltpu.VMEM((ROWS, WIDTH), bf16),
            pltpu.VMEM((ROWS, WIDTH), bf16),
            pltpu.VMEM((ROWS, WIDTH), jnp.float32),
            pltpu.VMEM((ROWS, WIDTH), bf16),
            pltpu.VMEM((ROWS, WIDTH), bf16),
            pltpu.VMEM((SEQ, PIECE, WIDTH), bf16),
            pltpu.VMEM((SEQ, PIECE, WIDTH), bf16),
            pltpu.VMEM((2, SEQ, PIECE, WIDTH), bf16),
            dma((6,)),
            dma((2, BLOCKS + 1)),
            dma((2, BLOCKS + 1)),
            dma((16,)),
            dma((16,)),
            dma((BLOCKS,)),
            dma((BLOCKS,)),
            dma((BLOCKS + 1,)),
            dma((BLOCKS + 1,)),
            dma((BLOCKS + 1,)),
            dma((BLOCKS + 1,)),
            dma((BLOCKS + 1,)),
            dma((BLOCKS + 1,)),
            dma((BLOCKS, PIECES)),
            dma((2,)),
            dma((2, SEQ)),
            dma((HALF,)),
            dma((BLOCKS,)),
        ],
        compiler_params=pltpu.CompilerParams(
            collective_id=0, has_side_effects=True, vmem_limit_bytes=56 * 1024 * 1024
        ),
        cost_estimate=pl.CostEstimate(
            flops=20_000_000_000, bytes_accessed=12_000_000, transcendentals=11_000_000
        ),
    )(doc_lengths, owner_of, queries, key_heads, token_value_heads, out_weight)


def solution(mesh):
    return jax.shard_map(
        body,
        mesh=mesh,
        in_specs=(P("seq", "tp"), P("seq", "tp"), P("seq", "tp"), P("tp", None), P(), P()),
        out_specs=P("seq", "tp"),
        check_vma=False,
    )
```

```python
import functools
import math

import jax
import jax.numpy as jnp
from jax import lax
from jax.experimental import pallas as pl
from jax.experimental.pallas import tpu as pltpu
from jax.sharding import PartitionSpec as P

HEAD_SIZE = 128
BLK = 128
LEN = 4096
MAXDOC = 2048
HEADS = 5
ROWS = 1024
WIDTH = HEADS * HEAD_SIZE
BLOCKS = ROWS // BLK
WINDOW = MAXDOC + BLK
SEQ = 32
TP = 8
PER_SEQ = LEN // ROWS
PIECES = 8
PIECE = BLK // PIECES
W_PIECE = 64
W_ROWS = 4 * WIDTH + 128
MESH = pl.DeviceIdType.MESH

HALF = BLOCKS // 2

D_FORWARD = 1
D_PROJ = 3
D_FINAL = 5
D_MID = 6


def block_at(place):
    late = jnp.where(place == 7, 0, 13 - 2 * place)
    return jnp.where(place < HALF, jnp.where(place == 0, 7, 8 - 2 * place), late)


def pair_of(z):
    return lax.rem(z + jnp.where(lax.rem(z, 2) == 1, 1, TP - 1), TP)


def buddy_of(z):
    return z + 1 - 2 * lax.rem(z, 2)


def far_of(z):
    return lax.rem(z + jnp.where(lax.rem(z, 2) == 1, 3, 5), TP)


def middle_of(place, piece):
    y = piece // 2
    x = 2 * (piece % 2) + lax.rem(y + place, 2)
    return (y * 4 + x) * 2 + lax.rem(place // 2, 2)


def kernel(
    doc_ref,
    owner_ref,
    q_hbm,
    k_hbm,
    v_hbm,
    w_hbm,
    out_ref,
    queries,
    kbuf,
    vbuf,
    probs,
    inverse_vmem,
    inverse_ref,
    weight,
    att,
    psend,
    precv,
    own_part,
    attended,
    mixed,
    midr_low,
    midr_high,
    mids,
    local_sem,
    kv_send,
    kv_recv,
    w_send,
    w_recv,
    own_send,
    own_recv,
    far_send,
    far_recv,
    forward_send,
    forward_recv,
    pair_send,
    pair_recv,
    route_send,
    mid_recv,
    mid_send,
    placed_recv,
    out_recv,
):
    midr = (midr_low, midr_high)
    me = lax.axis_index("seq")
    z = lax.axis_index("tp")
    core = lax.rem(me, 2)
    x = lax.rem(me // 2, 4)
    y = me // 8
    j = lax.rem(me, PER_SEQ)
    pair, buddy, far = pair_of(z), buddy_of(z), far_of(z)
    far_buddy = buddy_of(far)
    scale = math.log2(math.e) / math.sqrt(HEAD_SIZE)

    def remote(src, dst, send, recv, target):
        return pltpu.make_async_remote_copy(
            src_ref=src,
            dst_ref=dst,
            send_sem=send,
            recv_sem=recv,
            device_id=target,
            device_id_type=MESH,
        )

    own_k = pltpu.make_async_copy(k_hbm, kbuf.at[pl.ds(2 * ROWS, ROWS)], local_sem.at[0])
    own_v = pltpu.make_async_copy(v_hbm, vbuf.at[pl.ds(2 * ROWS, ROWS)], local_sem.at[1])
    own_q = pltpu.make_async_copy(q_hbm, queries, local_sem.at[4])
    own_k.start()
    own_q.start()
    own_v.start()

    def own_weight(half):
        column = pl.multiple_of((pair if half else z) * WIDTH, WIDTH)
        return pltpu.make_async_copy(
            w_hbm.at[:, pl.ds(column, WIDTH)],
            weight.at[pl.ds(0, WIDTH), pl.ds(half * WIDTH, WIDTH)],
            local_sem.at[2 + half],
        )

    for half in range(2):
        own_weight(half).start()

    barrier = pltpu.get_barrier_semaphore()

    @pl.loop(1, SEQ)
    def _(step):
        pl.semaphore_signal(
            barrier, inc=1, device_id={"seq": lax.rem(me + step, SEQ)}, device_id_type=MESH
        )

    for target in (pair, buddy, far, far_buddy):
        pl.semaphore_signal(barrier, inc=1, device_id={"tp": target}, device_id_type=MESH)

    block_no = lax.broadcasted_iota(jnp.int32, (8, 128), 0)
    owner_no = lax.broadcasted_iota(jnp.int32, (8, 128), 1)

    def add_index(index, inverse):
        for block in range(BLOCKS):
            here = (block_no == block) & (owner_no == owner_ref[index * BLOCKS + block])
            inverse = jnp.where(here, index, inverse)
        return inverse

    inverse_vmem[...] = lax.fori_loop(0, SEQ, add_index, jnp.zeros((8, 128), jnp.int32))
    to_scalars = pltpu.make_async_copy(inverse_vmem, inverse_ref, local_sem.at[5])
    to_scalars.start()
    pl.semaphore_wait(barrier, SEQ - 1 + 4)

    piece_no = (core * 4 + y) * 4 + x
    group = jnp.minimum(piece_no // 10, 2)
    w_target = jnp.where(group == 0, buddy, jnp.where(group == 1, far, far_buddy))

    def w_rows(yy, xx):
        start = WIDTH + ((core * 4 + yy) * 4 + xx) * W_PIECE
        return pl.ds(pl.multiple_of(start, W_PIECE), W_PIECE)

    def w_half(half):
        return pl.ds(half * WIDTH, WIDTH)

    def w_first(half):
        column = pair_of(w_target) if half else w_target
        src = w_hbm.at[
            pl.ds(pl.multiple_of(lax.rem(piece_no, 10) * W_PIECE, W_PIECE), W_PIECE),
            pl.ds(pl.multiple_of(column * WIDTH, WIDTH), WIDTH),
        ]
        dst = weight.at[w_rows(y, x), w_half(half)]
        return remote(src, dst, w_send.at[half], w_recv.at[half], {"tp": w_target})

    def along_x(hop):
        return {"seq": (y * 4 + lax.rem(x + hop, 4)) * 2 + core}

    def along_y(hop):
        return {"seq": (lax.rem(y + hop, 4) * 4 + x) * 2 + core}

    def w_second(half, hop):
        sem = 2 + half * 3 + hop - 1
        ref = weight.at[w_rows(y, x), w_half(half)]
        target = along_y(hop) if half else along_x(hop)
        return remote(ref, ref, w_send.at[sem], w_recv.at[sem], target)

    four_rows = pl.ds(pl.multiple_of(WIDTH + (core * 4 + y) * 4 * W_PIECE, W_PIECE), 4 * W_PIECE)

    def w_third(half, hop):
        sem = 8 + half * 3 + hop - 1
        ref = weight.at[four_rows, w_half(half)]
        target = along_x(hop) if half else along_y(hop)
        return remote(ref, ref, w_send.at[sem], w_recv.at[sem], target)

    def w_third_piece(hop, yy):
        sem = 11 + hop - 1
        ref = weight.at[w_rows(yy, x), w_half(1)]
        return remote(ref, ref, w_send.at[sem], w_recv.at[sem], along_x(hop))

    def w_fourth(half):
        sem = 14 + half
        rows = pl.ds(pl.multiple_of(WIDTH + core * 16 * W_PIECE, W_PIECE), 16 * W_PIECE)
        ref = weight.at[rows, w_half(half)]
        return remote(ref, ref, w_send.at[sem], w_recv.at[sem], {"seq": me + 1 - 2 * core})

    w_first(1).start()
    w_first(0).start()

    def near_kv(which):
        src, buf = ((k_hbm, kbuf), (v_hbm, vbuf))[which]
        return remote(
            src,
            buf.at[pl.ds(ROWS, ROWS)],
            kv_send.at[which, BLOCKS],
            kv_recv.at[which, BLOCKS],
            {"seq": lax.rem(me + 1, SEQ)},
        )

    def next_kv(which, piece):
        src, buf = ((k_hbm, kbuf), (v_hbm, vbuf))[which]
        rows = pl.ds(pl.multiple_of(piece * BLK, BLK), BLK)
        return remote(
            src.at[rows],
            buf.at[rows],
            kv_send.at[which, piece],
            kv_recv.at[which, piece],
            {"seq": lax.rem(me + 2, SEQ)},
        )

    for which in range(2):

        @pl.when(j < 3)
        def _():
            near_kv(which).start()

        @pl.when(j < 2)
        def _():
            next_kv(which, BLOCKS - 1).start()

    @pl.when(j < 2)
    def _():
        kbuf[pl.ds(0, ROWS), :] = jnp.zeros((ROWS, HEAD_SIZE), kbuf.dtype)
        vbuf[pl.ds(0, ROWS), :] = jnp.zeros((ROWS, HEAD_SIZE), vbuf.dtype)

    @pl.when(j < 1)
    def _():
        kbuf[pl.ds(ROWS, ROWS), :] = jnp.zeros((ROWS, HEAD_SIZE), kbuf.dtype)
        vbuf[pl.ds(ROWS, ROWS), :] = jnp.zeros((ROWS, HEAD_SIZE), vbuf.dtype)

    def rows_of(block):
        return pl.ds(pl.multiple_of(block * BLK, BLK), BLK)

    def slot(no):
        return pl.ds(no * WIDTH, WIDTH)

    def span(place, part):
        if part is None:
            return rows_of(place), place
        return pl.ds((BLOCKS - 1) * BLK + part * (BLK // 2), BLK // 2), BLOCKS - 1 + part

    def own_copy(block):
        rows = rows_of(block)
        return remote(
            att.at[rows, slot(0)],
            att.at[rows, slot(1)],
            own_send.at[block],
            own_recv.at[block],
            {"tp": buddy},
        )

    def far_copy(place, part=None):
        rows, sem = span(place, part)
        return remote(
            att.at[rows, slot(0)],
            att.at[rows, slot(2)],
            far_send.at[sem],
            far_recv.at[sem],
            {"tp": far},
        )

    def forward_copy(place, part=None):
        rows, sem = span(place, part)
        return remote(
            att.at[rows, slot(2)],
            att.at[rows, slot(3)],
            forward_send.at[sem],
            forward_recv.at[sem],
            {"tp": buddy},
        )

    def pair_copy(place, part=None):
        rows, sem = span(place, part)
        return remote(
            psend.at[rows], precv.at[rows], pair_send.at[sem], pair_recv.at[sem], {"tp": pair}
        )

    def wait_kv(step, block, which):
        @pl.when(step == 0)
        def _():
            (own_k, own_v)[which].wait()

        @pl.when((step == 0) & (j >= 1))
        def _():
            near_kv(which).wait_recv()

        @pl.when(j >= 2)
        def _():
            next_kv(which, block).wait_recv()

    def attention(step, place):
        block = block_at(place)
        rows = rows_of(block)
        window = pl.ds(pl.multiple_of(block * BLK, BLK), WINDOW)
        wait_kv(step, block, 0)
        keys = kbuf[window, :]
        base = j * ROWS + block * BLK
        position = base + lax.broadcasted_iota(jnp.int32, (BLK, 1), 0)
        bound = jnp.int32(0)
        first = jnp.zeros((BLK, 1), jnp.int32)
        for doc in range(doc_ref.shape[1]):
            bound = bound + doc_ref[me // PER_SEQ, doc]
            first = jnp.where(position >= bound, bound, first)
        first = first - base + MAXDOC
        key_no = lax.broadcasted_iota(jnp.int32, (BLK, WINDOW), 1)
        last = MAXDOC + lax.broadcasted_iota(jnp.int32, (BLK, WINDOW), 0)
        allowed = (key_no >= first) & (key_no <= last)
        totals = []
        for head in range(HEADS):
            columns = pl.ds(head * HEAD_SIZE, HEAD_SIZE)
            scores = lax.dot_general(
                queries[rows, columns],
                keys,
                (((1,), (1,)), ((), ())),
                preferred_element_type=jnp.float32,
            )
            scores = jnp.where(allowed, scores * scale, -1e30)
            weights = jnp.exp2(scores - jnp.max(scores, axis=1, keepdims=True))
            totals.append(jnp.sum(weights, axis=1, keepdims=True))
            probs[pl.ds(head * BLK, BLK), :] = weights.astype(jnp.bfloat16)
        wait_kv(step, block, 1)
        mix = jnp.dot(probs[...], vbuf[window, :], preferred_element_type=jnp.float32)
        for head in range(HEADS):
            part = mix[head * BLK : (head + 1) * BLK] / totals[head]
            columns = pl.ds(head * HEAD_SIZE, HEAD_SIZE)
            attended[rows_of(place), columns] = part.astype(jnp.bfloat16)

    def project(rows, half):
        return jnp.dot(
            att[rows, :],
            weight[pl.ds(0, 4 * WIDTH), pl.ds(half * WIDTH, WIDTH)],
            preferred_element_type=jnp.float32,
        )

    def route_copy(place, piece, role, target):
        rows = pl.ds(pl.multiple_of(place * BLK + piece * PIECE, PIECE), PIECE)
        return remote(
            (mixed, attended)[role].at[rows],
            midr[role].at[me],
            route_send.at[place, piece],
            mid_recv.at[role],
            {"seq": target},
        )

    my_piece = y * 2 + x // 2

    def my_place(role):
        return lax.rem(x + y, 2) + 2 * core + HALF * role

    def piece_rows(block):
        return pl.ds(pl.multiple_of(block * BLK + my_piece * PIECE, PIECE), PIECE)

    def mid_target(role):
        place = my_place(role)
        if role == 0:
            return out_ref.at[piece_rows(block_at(place))], out_recv.at[place]
        return att.at[piece_rows(place), slot(0)], placed_recv.at[place - HALF]

    def mid_copy(role, target):
        dst, sem = mid_target(role)
        return remote(
            mids.at[role, target], dst, mid_send.at[role, target], sem, {"seq": target}
        )

    def own_mid(role):
        src = (mixed, attended)[role].at[piece_rows(my_place(role))]
        return pltpu.make_async_copy(src, midr[role].at[me], mid_recv.at[role])

    def own_out(role):
        dst, sem = mid_target(role)
        return pltpu.make_async_copy(mids.at[role, me], dst, sem)

    def route(place, role):
        for piece in range(PIECES):
            target = middle_of(place, piece)

            @pl.when(target != me)
            def _():
                route_copy(place, piece, role, target).start()

        @pl.when(place == my_place(role))
        def _():
            own_mid(role).start()

    def reorder(place, role):
        @pl.when(place == my_place(role))
        def _():
            pltpu.make_async_copy(midr[role], midr[role], mid_recv.at[role]).wait()
            block = block_at(place)

            @pl.loop(0, SEQ)
            def _(owner):
                mids[role, owner] = midr[role][inverse_ref[block, owner]]

                @pl.when(owner != me)
                def _():
                    mid_copy(role, owner).start()

                @pl.when(owner == me)
                def _():
                    own_out(role).start()

    def placed_wait(place):
        ref = att.at[rows_of(place), slot(0)]
        pltpu.make_async_copy(ref, ref, placed_recv.at[place - HALF]).wait()

    def own_result(place, part=None):
        rows = span(place, part)[0]
        if part is None:
            out_rows = rows_of(block_at(place))
        else:
            out_rows = pl.ds(part * (BLK // 2), BLK // 2)
        return pltpu.make_async_copy(
            mixed.at[rows], out_ref.at[out_rows], out_recv.at[place]
        )

    def parts_of(place):
        return [
            lambda f: pl.when(place < BLOCKS - 1)(lambda: f(None)),
            lambda f: pl.when(place == BLOCKS - 1)(lambda: (f(0), f(1))[0]),
        ]

    @pl.loop(0, BLOCKS + D_FINAL)
    def _(step):
        @pl.when(step == 0)
        def _():
            own_q.wait()
            to_scalars.wait()

        @pl.when(step == 1)
        def _():
            for half in (1, 0):
                w_first(half).wait_recv()
                for hop in (1, 3, 2):
                    w_second(half, hop).start()

            @pl.when(j < 2)
            def _():
                @pl.loop(1, BLOCKS)
                def _(back):
                    next_kv(0, BLOCKS - 1 - back).start()
                    next_kv(1, BLOCKS - 1 - back).start()

        @pl.when(step == 2)
        def _():
            for hop in (1, 3, 2):
                w_second(1, hop).wait_recv()
            for hop in (1, 3, 2):
                for yy in range(4):
                    w_third_piece(hop, yy).start()
            for hop in (1, 3, 2):
                w_second(0, hop).wait_recv()
            for hop in (1, 3, 2):
                w_third(0, hop).start()

        @pl.when((step >= HALF) & (step < BLOCKS))
        def _():
            placed_wait(step)
            for part in parts_of(step):

                @part
                def _(number):
                    far_copy(step, number).start()

            own_copy(step).start()

        @pl.loop(0, 2)
        def _(late):
            place = jnp.where(late == 1, step + HALF - 1, step)
            first_step = late

            @pl.when((step >= first_step) & (step < first_step + HALF))
            def _():
                attention(step, place)

                @pl.when(late == 0)
                def _():
                    rows = rows_of(place)
                    att[rows, slot(0)] = attended[rows, :]
                    far_copy(place).start()
                    own_copy(place).start()

                @pl.when(late == 1)
                def _():
                    route(place, 1)

        @pl.when((step >= D_FORWARD) & (step < D_FORWARD + BLOCKS))
        def _():
            place = step - D_FORWARD
            for part in parts_of(place):

                @part
                def _(number):
                    far_copy(place, number).wait_recv()
                    forward_copy(place, number).start()

        @pl.when(step == 3)
        def _():
            for half in (1, 0):
                for hop in (1, 3, 2):
                    w_third(half, hop).wait_recv()
                w_fourth(half).start()

        reorder(step + 2, 1)

        @pl.when(step == D_PROJ)
        def _():
            own_weight(1).wait()
            w_fourth(1).wait_recv()

        @pl.when((step >= D_PROJ) & (step < D_PROJ + BLOCKS))
        def _():
            place = step - D_PROJ
            own_copy(place).wait_recv()
            for part in parts_of(place):

                @part
                def _(number):
                    rows = span(place, number)[0]
                    forward_copy(place, number).wait_recv()
                    psend[rows, :] = project(rows, 1).astype(jnp.bfloat16)
                    pair_copy(place, number).start()

            @pl.when(place == 0)
            def _():
                own_weight(0).wait()
                w_fourth(0).wait_recv()

            rows = rows_of(place)
            own_part[rows, :] = project(rows, 0)

        @pl.when((step >= D_FINAL) & (step < D_FINAL + BLOCKS))
        def _():
            place = step - D_FINAL
            for part in parts_of(place):

                @part
                def _(number):
                    rows = span(place, number)[0]
                    pair_copy(place, number).wait_recv()
                    mixed[rows, :] = (
                        own_part[rows, :] + precv[rows, :].astype(jnp.float32)
                    ).astype(jnp.bfloat16)

                    @pl.when(place >= HALF)
                    def _():
                        own_result(place, number).start()

            @pl.when(place < HALF)
            def _():
                route(place, 0)

        reorder(step - D_MID, 0)

    for block in range(BLOCKS):
        rows = pl.ds(block * BLK, BLK)
        pltpu.make_async_copy(out_ref.at[rows], out_ref.at[rows], out_recv.at[block]).wait()

    @pl.when(j < 3)
    def _():
        near_kv(0).wait_send()
        near_kv(1).wait_send()

    @pl.when(j < 2)
    def _():
        @pl.loop(0, BLOCKS)
        def _(piece):
            next_kv(0, piece).wait_send()
            next_kv(1, piece).wait_send()

    for half in range(2):
        w_first(half).wait_send()
        w_fourth(half).wait_send()
        for hop in (1, 2, 3):
            w_second(half, hop).wait_send()
            w_third(half, hop).wait_send()

    @pl.loop(0, BLOCKS)
    def _(block):
        own_copy(block).wait_send()
        for part in parts_of(block):

            @part
            def _(number):
                far_copy(block, number).wait_send()
                forward_copy(block, number).wait_send()
                pair_copy(block, number).wait_send()

        for piece in range(PIECES):
            target = middle_of(block, piece)

            @pl.when(target != me)
            def _():
                route_copy(block, piece, 0, target).wait_send()

    @pl.loop(0, SEQ)
    def _(owner):
        @pl.when(owner != me)
        def _():
            mid_copy(0, owner).wait_send()
            mid_copy(1, owner).wait_send()


def body(queries, key_heads, token_value_heads, out_weight, doc_lengths, owner_of):
    dma = pltpu.SemaphoreType.DMA
    bf16 = jnp.bfloat16
    any_space = pl.BlockSpec(memory_space=pl.ANY)
    smem = pl.BlockSpec(memory_space=pltpu.SMEM)
    return pl.pallas_call(
        kernel,
        out_shape=jax.ShapeDtypeStruct((ROWS, WIDTH), bf16),
        in_specs=[smem, smem] + [any_space] * 4,
        out_specs=any_space,
        scratch_shapes=[
            pltpu.VMEM((ROWS, WIDTH), bf16),
            pltpu.VMEM((3 * ROWS, HEAD_SIZE), bf16),
            pltpu.VMEM((3 * ROWS, HEAD_SIZE), bf16),
            pltpu.VMEM((HEADS * BLK, WINDOW), bf16),
            pltpu.VMEM((8, 128), jnp.int32),
            pltpu.SMEM((8, 128), jnp.int32),
            pltpu.VMEM((W_ROWS, 2 * WIDTH), bf16),
            pltpu.VMEM((ROWS, 4 * WIDTH), bf16),
            pltpu.VMEM((ROWS, WIDTH), bf16),
            pltpu.VMEM((ROWS, WIDTH), bf16),
            pltpu.VMEM((ROWS, WIDTH), jnp.float32),
            pltpu.VMEM((ROWS, WIDTH), bf16),
            pltpu.VMEM((ROWS, WIDTH), bf16),
            pltpu.VMEM((SEQ, PIECE, WIDTH), bf16),
            pltpu.VMEM((SEQ, PIECE, WIDTH), bf16),
            pltpu.VMEM((2, SEQ, PIECE, WIDTH), bf16),
            dma((6,)),
            dma((2, BLOCKS + 1)),
            dma((2, BLOCKS + 1)),
            dma((16,)),
            dma((16,)),
            dma((BLOCKS,)),
            dma((BLOCKS,)),
            dma((BLOCKS + 1,)),
            dma((BLOCKS + 1,)),
            dma((BLOCKS + 1,)),
            dma((BLOCKS + 1,)),
            dma((BLOCKS + 1,)),
            dma((BLOCKS + 1,)),
            dma((BLOCKS, PIECES)),
            dma((2,)),
            dma((2, SEQ)),
            dma((HALF,)),
            dma((BLOCKS,)),
        ],
        compiler_params=pltpu.CompilerParams(
            collective_id=0, has_side_effects=True, vmem_limit_bytes=56 * 1024 * 1024
        ),
        cost_estimate=pl.CostEstimate(
            flops=20_000_000_000, bytes_accessed=12_000_000, transcendentals=11_000_000
        ),
    )(doc_lengths, owner_of, queries, key_heads, token_value_heads, out_weight)


def solution(mesh):
    return jax.shard_map(
        body,
        mesh=mesh,
        in_specs=(P("seq", "tp"), P("seq", "tp"), P("seq", "tp"), P("tp", None), P(), P()),
        out_specs=P("seq", "tp"),
        check_vma=False,
    )
```
